256 devices in a mesh: nodes: 64 (over y, z, core), mp: 4 (over x).
Axes of the slice: x: 4, y: 4, z: 8, core: 2. Of those that a mesh axis runs over, the one named last changes fastest.
Arguments:
- input_history: float32 [262144, 512], P('nodes', 'mp'), may hold values from -6 to 6
- hidden_history: float32 [262144, 512], P('nodes', 'mp'), may hold values from -6 to 6
- batch_blocks: int32 [64, 24], P('nodes'), may hold values from 0 to 31, as said below
- tile_columns: int32 [1536, 5], P('nodes'), may hold values from 0 to 215, as said below
- tile_values: bfloat16 [1536, 5, 128, 128], P('nodes'), may hold values from -0.25 to 0.25
- send_blocks: int32 [64, 64, 3], P('nodes'), may hold values from 0 to 31
- send_counts: int32 [64, 64], P('nodes'), may hold values from 2 to 3
- weight_first: bfloat16 [512, 512], P('mp'), may hold values from -0.25 to 0.25
- weight_second: bfloat16 [512, 512], P('mp'), may hold values from -0.25 to 0.25
- cotangent: bfloat16 [196608, 512], P('nodes', 'mp'), may hold values from -0.0134887695 to 0.0134887695
Outputs:
- layer_out: bfloat16 [196608, 512], P('nodes', 'mp')
- grad_first: float32 [512, 512], P('mp')
- grad_second: float32 [512, 512], P('mp')
The draws below stay inside these ranges and needn't reach their ends.
Inputs may be any that keep to these rules, and one draw needn't show every extreme that they name: `batch_blocks`: the 24 blocks of one partition are different. `tile_columns`: column 0 of each row is the row's own block i, column 1 is a batch block below 24; columns 2 to 4 are halo slots 24 + o * 3 + j.
All inputs are finite; a program needn't handle non-finite values.
Results may differ from the reference program's by a relative error of at most 0.012.
Values may be sent and summed in bfloat16 or wider, within the bound.
No kernel may reach another device: no remote copies, remote signals or barrier semaphores. Data moves between devices by JAX's collectives and lax.ppermute only.
A program may use at most 128 MiB of HBM per device.

```python
import jax
import jax.numpy as jnp
from jax import lax

D = 512
BS = 128
NB = 24
TPR = 5
CAP = 3
HB = 32
ROWS = 196608
HIST_ROWS = 262144
N_NODES = 64


def draw_batch_blocks(key, part):
    key = jax.random.fold_in(key, 23)
    keys = jax.random.split(key, N_NODES)

    def one_device(device_key):
        return jax.random.permutation(device_key, HB)[:NB].astype(jnp.int32)
    return jax.vmap(one_device)(keys)


def draw_tile_columns(key, part):
    key = jax.random.fold_in(key, 11)
    keys = jax.random.split(key, 3)
    total = N_NODES * NB
    positions = jnp.arange(total, dtype=jnp.int32)
    device = positions // NB
    own = positions % NB
    other = jax.random.randint(keys[0], (total,), 0, NB).astype(jnp.int32)
    offset = jax.random.randint(keys[1], (total, TPR - 2), 0, N_NODES).astype(jnp.int32)
    owner = (device[:, None] + offset) % N_NODES
    slot = jax.random.randint(keys[2], (total, TPR - 2), 0, CAP).astype(jnp.int32)
    halo = NB + owner * CAP + slot
    return jnp.concatenate([own[:, None], other[:, None], halo], axis=1).astype(jnp.int32)


def touch_ends(result, key, least, high):
    index_at = [jax.random.randint(jax.random.fold_in(key, axis), (), 0, length) for axis, length in enumerate(result.shape)]
    longest = result.shape.index(max(result.shape))
    beside = index_at[:longest] + [(index_at[longest] + 1) % result.shape[longest]] + index_at[longest + 1:]
    return result.at[tuple(index_at)].set(least).at[tuple(beside)].set(high)


def shard_levels(own_key, shape, cuts, least, top_value):
    factor_of = 1.0
    for dim, parts in cuts:
        draws = jax.random.uniform(jax.random.fold_in(jax.random.fold_in(own_key, 6), dim), (parts,), jnp.float32, least / len(cuts), top_value / len(cuts))
        factor_of = factor_of * jnp.repeat(jnp.exp(draws), shape[dim] // parts).reshape((-1,) + (1,) * (len(shape) - 1 - dim))
    return factor_of


def normal_values(key, extent, deviation, limit, cuts=(), held_as=jnp.bfloat16):
    loudness = shard_levels(key, extent, cuts, -0.22, 0.18) if cuts else 1.0
    array = jax.random.normal(key, extent, jnp.float32) * deviation * loudness
    return jnp.minimum(jnp.maximum(array, -limit), limit).astype(held_as)


def setup_inputs(seed: int = 0) -> dict:
    key_of = jax.random.split(jax.random.key(seed), 11)
    input_history = normal_values(key_of[0], (HIST_ROWS, D), 1.0, 6.0, ((0, 64), (1, 4)), jnp.float32)
    hidden_history = normal_values(key_of[1], (HIST_ROWS, D), 1.0, 6.0, ((0, 64), (1, 4)), jnp.float32)
    batch_blocks = draw_batch_blocks(jax.random.fold_in(key_of[10], 71), 0)
    tile_columns = draw_tile_columns(jax.random.fold_in(key_of[10], 71), 0)
    tile_values = normal_values(key_of[4], (N_NODES * NB, TPR, BS, BS), (BS * TPR) ** -0.5, 0.25, ((0, 64),))
    send_blocks = touch_ends(jax.random.randint(key_of[5], (N_NODES, N_NODES, CAP), 0, HB), jax.random.fold_in(key_of[5], 1), 0, HB - 1).astype(jnp.int32)
    send_counts = touch_ends(jax.random.randint(key_of[6], (N_NODES, N_NODES), CAP - 1, CAP + 1), jax.random.fold_in(key_of[6], 1), CAP - 1, CAP).astype(jnp.int32)
    weight_first = normal_values(key_of[7], (D, D), D ** -0.5, 0.25, ((0, 4),))
    weight_second = normal_values(key_of[8], (D, D), D ** -0.5, 0.25, ((0, 4),))
    cotangent = normal_values(key_of[9], (ROWS, D), (1.0 / (NB * BS * N_NODES) ** 0.5), 0.0134887695, ((0, 64), (1, 4)))
    return dict(input_history=input_history, hidden_history=hidden_history, batch_blocks=batch_blocks, tile_columns=tile_columns, tile_values=tile_values, send_blocks=send_blocks, send_counts=send_counts, weight_first=weight_first, weight_second=weight_second, cotangent=cotangent)


def slope(value):
    sig = jax.nn.sigmoid(value)
    return sig * (1.0 + value * (1.0 - sig))


def aggregate(local, halo, tiles, columns):
    source = jnp.concatenate([local, halo], axis=0)
    picked = source[columns]
    summed = jnp.einsum('rtij,rtjc->ric', tiles.astype(jnp.float32), picked.astype(jnp.float32))
    return summed.astype(jnp.bfloat16).reshape(-1, local.shape[2])


def spread_back(back_rows, tiles, columns):
    width = back_rows.shape[1]
    blocks = back_rows.reshape(NB, BS, width).astype(jnp.float32)
    contrib = jnp.einsum('rtji,rjc->rtic', tiles[:, :2].astype(jnp.float32), blocks)
    onehot = (columns[:, :2][None, :, :] == jnp.arange(NB, dtype=jnp.int32)[:, None, None]).astype(jnp.float32)
    return jnp.einsum('krt,rtic->kic', onehot, contrib, precision=lax.Precision.HIGHEST).reshape(NB * BS, width)


def reference(input_history, hidden_history, batch_blocks, tile_columns, tile_values, send_blocks, send_counts, weight_first, weight_second, cotangent):
    peers = send_counts.shape[0]
    width = input_history.shape[1]
    table_input = input_history.reshape(peers, HB, BS, width)
    table_hidden = hidden_history.reshape(peers, HB, BS, width)
    tiles_all = tile_values.reshape(peers, NB, TPR, BS, BS)
    columns_all = tile_columns.reshape(peers, NB, TPR)
    cot_all = cotangent.reshape(peers, NB * BS, width)
    owners = jnp.arange(peers, dtype=jnp.int32)
    slot_ids = jnp.arange(CAP, dtype=jnp.int32)

    def pull(table, reader):
        wanted = send_blocks[:, reader, :]
        blocks = table[owners[:, None], wanted]
        live = slot_ids[None, :] < send_counts[:, reader][:, None]
        blocks = jnp.where(live[:, :, None, None], blocks, jnp.zeros_like(blocks))
        return blocks.astype(jnp.bfloat16).reshape(peers * CAP, BS, width)

    def step(carry, reader):
        total_first, total_second = carry
        tiles = tiles_all[reader]
        columns = columns_all[reader]
        local = table_input[reader][batch_blocks[reader]].astype(jnp.bfloat16)
        summed_first = aggregate(local, pull(table_input, reader), tiles, columns)
        pre_first = jnp.dot(summed_first, weight_first, preferred_element_type=jnp.float32)
        hidden_first = jax.nn.silu(pre_first).astype(jnp.bfloat16)
        summed_second = aggregate(hidden_first.reshape(NB, BS, width), pull(table_hidden, reader), tiles, columns)
        pre_second = jnp.dot(summed_second, weight_second, preferred_element_type=jnp.float32)
        layer_out = jax.nn.silu(pre_second).astype(jnp.bfloat16)
        delta_second = (cot_all[reader].astype(jnp.float32) * slope(pre_second)).astype(jnp.bfloat16)
        total_second = total_second + jnp.dot(summed_second.T, delta_second, preferred_element_type=jnp.float32)
        back_second = jnp.dot(delta_second, weight_second.T, preferred_element_type=jnp.float32).astype(jnp.bfloat16)
        back_hidden = spread_back(back_second, tiles, columns)
        delta_first = (back_hidden * slope(pre_first)).astype(jnp.bfloat16)
        total_first = total_first + jnp.dot(summed_first.T, delta_first, preferred_element_type=jnp.float32)
        return (total_first, total_second), layer_out

    start = (jnp.zeros((width, width), jnp.float32), jnp.zeros((width, width), jnp.float32))
    (grad_first, grad_second), outs = lax.scan(step, start, jnp.arange(peers, dtype=jnp.int32))
    return outs.reshape(peers * NB * BS, width), grad_first, grad_second
```

```python
import functools

import jax
import jax.numpy as jnp
from jax import lax
from jax.experimental import pallas as pl
from jax.experimental.pallas import tpu as pltpu
from jax.sharding import Mesh
from jax.sharding import PartitionSpec as P

Y, Z, C, X = 4, 8, 2, 4
G = Y * C
BS = 128
NB = 24
TPR = 5
CAP = 3
HB = 32
ROWS = NB * BS
QUARTER = ROWS // X
STEP = 4
F32 = jnp.float32
BF16 = jnp.bfloat16
ANY = pl.BlockSpec(memory_space=pltpu.HBM)
VMEM = pl.BlockSpec(memory_space=pltpu.VMEM)
SMEM = pl.BlockSpec(memory_space=pltpu.SMEM)
LIMIT = 48 * 1024 * 1024


def call(kernel, out_shape, in_specs, out_specs, scratch, cost, name):
    return pl.pallas_call(
        kernel,
        out_shape=out_shape,
        in_specs=in_specs,
        out_specs=out_specs,
        scratch_shapes=scratch,
        compiler_params=pltpu.CompilerParams(vmem_limit_bytes=LIMIT),
        cost_estimate=pl.CostEstimate(flops=cost[0], bytes_accessed=cost[1], transcendentals=cost[2]),
        name=name,
    )


HEAD = 16
HALF = HB // 2
MIDDLE = HEAD + HALF * BS


def pack_kernel(blocks_ref, counts_ref, history_ref, after_ref, out_ref, wanted):
    del after_ref
    wanted[...] = jnp.zeros_like(wanted)
    blocks = blocks_ref[...]
    slot = lax.broadcasted_iota(jnp.int32, blocks.shape, 0)
    wanted[0:CAP, 0 : blocks.shape[1]] = jnp.where(slot < counts_ref[...], blocks, HB)
    out_ref[0:HEAD, :] = wanted[...].astype(F32).astype(BF16)

    def one(block, carry):
        rows = pl.multiple_of(block * BS, BS)
        out_ref[pl.ds(pl.multiple_of(HEAD + rows, HEAD), BS), :] = history_ref[pl.ds(rows, BS), :].astype(BF16)
        return carry

    lax.fori_loop(0, HB, one, 0)


def pack(blocks, counts, history, after):
    return call(
        pack_kernel,
        jax.ShapeDtypeStruct((HEAD + HB * BS, BS), BF16),
        [VMEM, VMEM, VMEM, ANY],
        VMEM,
        [pltpu.VMEM((HEAD, BS), jnp.int32)],
        (0, 3 * 1024 * 1024, 0),
        "pack",
    )(blocks, counts, history, after)


def stage_kernel(sizes, z_ref, *refs):
    count = len(sizes)
    total = sum(sizes)
    flat, (after_ref, out_ref, zeros, ints, asked, sem, head_sem) = refs[:total], refs[total:]
    del after_ref
    sources = [flat[sum(sizes[:s]) : sum(sizes[: s + 1])] for s in range(count)]
    for s in range(count):
        ints[s] = sources[s][0][0:HEAD, :].astype(F32).astype(jnp.int32)
        pltpu.make_async_copy(ints.at[s], asked.at[s], head_sem.at[s]).start()
    zeros[...] = jnp.zeros_like(zeros)
    for s in range(count):
        pltpu.make_async_copy(ints.at[s], asked.at[s], head_sem.at[s]).wait()
    mine = z_ref[0]

    def one(reader, carry):
        column = (reader // C) * (Z * C) + mine * C + lax.rem(reader, C)
        for s, source in enumerate(sources):
            limit = HB if len(source) == 1 else HALF
            for slot in range(CAP):
                block = asked[s, slot, column]
                target = out_ref.at[(reader * count + s) * CAP + slot]
                start = pl.multiple_of(HEAD + jnp.where(block < limit, block, 0) * BS, HEAD)

                @pl.when(block < limit)
                def _(source=source, start=start, target=target):
                    pltpu.make_async_copy(source[0].at[pl.ds(start, BS)], target, sem).start()

                if len(source) == 2:
                    late = jnp.logical_and(block >= HALF, block < HB)
                    begin = pl.multiple_of(jnp.where(late, block - HALF, 0) * BS, BS)

                    @pl.when(late)
                    def _(source=source, begin=begin, target=target):
                        pltpu.make_async_copy(source[1].at[pl.ds(begin, BS)], target, sem).start()

                @pl.when(block >= HB)
                def _(target=target):
                    pltpu.make_async_copy(zeros, target, sem).start()

        return carry

    lax.fori_loop(0, G, one, 0)
    pltpu.make_async_copy(out_ref, out_ref, sem).wait()


def stage(my_z, sources, after):
    count = len(sources)
    sizes = tuple(len(source) for source in sources)
    entries = G * CAP * count
    return call(
        functools.partial(stage_kernel, sizes),
        jax.ShapeDtypeStruct((entries, BS, BS), BF16),
        [SMEM] + [VMEM] * sum(sizes) + [ANY],
        ANY,
        [
            pltpu.VMEM((BS, BS), BF16),
            pltpu.VMEM((count, HEAD, BS), jnp.int32),
            pltpu.SMEM((count, HEAD, BS), jnp.int32),
            pltpu.SemaphoreType.DMA,
            pltpu.SemaphoreType.DMA((count,)),
        ],
        (0, 2 * entries * BS * BS * 2, 0),
        "stage",
    )(my_z, *[part for source in sources for part in source], after)


def aggregate_kernel(count, skip, local_ref, piece_ref, offset_ref, table_ref, *refs):
    halos, refs = refs[:count], refs[count:]
    tiles_ref, after_ref, out_ref, table, halo, tiles, table_sem, halo_sem, tiles_sem = refs
    del after_ref
    copy = pltpu.make_async_copy(table_ref.at[pl.ds(skip, table.shape[0])], table, table_sem)
    copy.start()

    def start(row, carry):
        pltpu.make_async_copy(tiles_ref.at[row], tiles.at[row], tiles_sem.at[row // STEP]).start()
        for slot in range(TPR - 2):
            use = row * (TPR - 2) + slot
            piece = piece_ref[use]
            offset = offset_ref[use]
            for number, source in enumerate(halos):

                @pl.when(piece == number)
                def _(source=source, slot=slot):
                    pltpu.make_async_copy(source.at[offset], halo.at[row, slot], halo_sem.at[row // STEP]).start()

        return carry

    lax.fori_loop(0, NB, start, 0)
    copy.wait()

    def compute(group, carry):
        rows = pl.ds(group * STEP, STEP)
        pltpu.make_async_copy(tiles_ref.at[rows], tiles.at[rows], tiles_sem.at[group]).wait()
        pltpu.make_async_copy(halo.at[rows], halo.at[rows], halo_sem.at[group]).wait()
        for k in range(STEP):
            row = group * STEP + k
            left = jnp.concatenate([tiles[row, t] for t in range(TPR)], axis=1)
            right = jnp.concatenate(
                [table[pl.ds(pl.multiple_of(local_ref[2 * row + t] * BS, BS), BS), :] for t in range(2)]
                + [halo[row, t] for t in range(TPR - 2)],
                axis=0,
            )
            summed = jnp.dot(left, right, preferred_element_type=F32)
            out_ref[pl.ds(pl.multiple_of(row * BS, BS), BS), :] = summed.astype(BF16)
        return carry

    lax.fori_loop(0, NB // STEP, compute, 0)


def aggregate(skip, table, halos, tiles, local, piece, offset, after):
    return call(
        functools.partial(aggregate_kernel, len(halos), skip),
        jax.ShapeDtypeStruct((ROWS, BS), BF16),
        [SMEM] * 3 + [ANY] * (len(halos) + 3),
        VMEM,
        [
            pltpu.VMEM((table.shape[0] - skip, BS), BF16),
            pltpu.VMEM((NB, TPR - 2, BS, BS), BF16),
            pltpu.VMEM((NB, TPR, BS, BS), BF16),
            pltpu.SemaphoreType.DMA,
            pltpu.SemaphoreType.DMA((NB // STEP,)),
            pltpu.SemaphoreType.DMA((NB // STEP,)),
        ],
        (2 * NB * TPR * BS**3, 2 * NB * TPR * BS * BS * 2, 0),
        "aggregate",
    )(local, piece, offset, table, *halos, tiles, after)


def sigmoid(value):
    return 1.0 / (1.0 + jnp.exp(-value))


def first_kernel(s0, s1, s2, far0, far1, weight_ref, hidden_ref, slope_ref):
    weight = weight_ref[...]
    step = 256
    half = ROWS // 2 // step

    def one(far, begin, row, carry):
        rows = pl.ds(pl.multiple_of((row + begin) * step, step), step)
        far_rows = pl.ds(pl.multiple_of(row * step, step), step)
        left = jnp.concatenate([s0[rows, :], s1[rows, :], s2[rows, :], far[far_rows, :]], axis=1)
        pre = jnp.dot(left, weight, preferred_element_type=F32)
        sig = sigmoid(pre)
        hidden_ref[rows, :] = (pre * sig).astype(BF16)
        slope_ref[rows, :] = sig * (1.0 + pre * (1.0 - sig))
        return carry

    lax.fori_loop(0, half, functools.partial(one, far0, 0), 0)
    lax.fori_loop(0, half, functools.partial(one, far1, half), 0)


def first_layer(summed, weight):
    return call(
        first_kernel,
        (jax.ShapeDtypeStruct((ROWS, BS), BF16), jax.ShapeDtypeStruct((ROWS, BS), F32)),
        [VMEM] * 6,
        (VMEM, VMEM),
        [],
        (2 * ROWS * 512 * BS, 6 * 1024 * 1024, ROWS * BS),
        "first_layer",
    )(*summed, weight)


def second_kernel(summed_ref, weight_ref, cot_ref, out_ref, delta_ref, back_ref):
    step = 128

    def one(row, carry):
        rows = pl.ds(pl.multiple_of(row * step, step), step)
        left = jnp.concatenate([summed_ref[k, rows, :] for k in range(X)], axis=1)
        cot = jnp.concatenate([cot_ref[k, rows, :] for k in range(X)], axis=1)
        pre = jnp.dot(left, weight_ref[...], preferred_element_type=F32)
        sig = sigmoid(pre)
        out = (pre * sig).astype(BF16)
        delta = (cot.astype(F32) * (sig * (1.0 + pre * (1.0 - sig)))).astype(BF16)
        back = lax.dot_general(
            delta, weight_ref[...], (((1,), (1,)), ((), ())), preferred_element_type=F32
        ).astype(BF16)
        delta_ref[rows, :] = delta
        for k in range(X):
            out_ref[k, rows, :] = out[:, k * BS : (k + 1) * BS]
            back_ref[k, rows, :] = back[:, k * BS : (k + 1) * BS]
        return carry

    lax.fori_loop(0, QUARTER // step, one, 0)


def second_layer(summed, weight, cot):
    piece = jax.ShapeDtypeStruct((X, QUARTER, BS), BF16)
    return call(
        second_kernel,
        (piece, jax.ShapeDtypeStruct((QUARTER, X * BS), BF16), piece),
        [VMEM] * 3,
        (VMEM,) * 3,
        [],
        (4 * QUARTER * 512 * 512, 5 * 1024 * 1024, QUARTER * 512),
        "second_layer",
    )(summed, weight, cot)


def grad_second_kernel(summed_ref, delta_ref, out_ref):
    for k in range(X):
        out_ref[k * BS : (k + 1) * BS, :] = lax.dot_general(
            summed_ref[k], delta_ref[...], (((0,), (0,)), ((), ())), preferred_element_type=F32
        ).astype(BF16)


def grad_second_part(summed, delta):
    return call(
        grad_second_kernel,
        jax.ShapeDtypeStruct((X * BS, X * BS), BF16),
        [VMEM] * 2,
        VMEM,
        [],
        (2 * QUARTER * 512 * 512, 3 * 1024 * 1024, 0),
        "grad_second",
    )(summed, delta)


def prepare_kernel(x_ref, tiles_ref, s0, s1, s2, far0, far1, turned_ref, summed_ref, tiles, sem):
    def start(row, carry):
        pltpu.make_async_copy(tiles_ref.at[row, pl.ds(0, 2)], tiles.at[row], sem).start()
        return carry

    lax.fori_loop(0, NB, start, 0)
    x = x_ref[0]
    half = ROWS // 2
    for source, step, begin in ((s0, 0, 0), (s1, X - 1, 0), (s2, 1, 0), (far0, 2, 0), (far1, 2, half)):
        place = pl.ds(pl.multiple_of(lax.rem(x + step, X) * BS, BS), BS)

        def one(block, carry, source=source, begin=begin, place=place):
            rows = pl.ds(pl.multiple_of(block * BS, BS), BS)
            columns = pl.ds(pl.multiple_of(begin + block * BS, BS), BS)
            summed_ref[place, columns] = source[rows, :].T
            return carry

        lax.fori_loop(0, source.shape[0] // BS, one, 0, unroll=4)
    pltpu.make_async_copy(tiles, tiles, sem).wait()

    def turn_tiles(row, carry):
        for t in range(2):
            turned_ref[row, pl.ds(t * BS, BS), :] = tiles[row, t].T
        return carry

    lax.fori_loop(0, NB, turn_tiles, 0, unroll=2)


def prepare(my_x, tiles, summed):
    return call(
        prepare_kernel,
        (jax.ShapeDtypeStruct((NB, 2 * BS, BS), BF16), jax.ShapeDtypeStruct((X * BS, ROWS), BF16)),
        [SMEM, ANY] + [VMEM] * 5,
        (VMEM, VMEM),
        [pltpu.VMEM((NB, 2, BS, BS), BF16), pltpu.SemaphoreType.DMA],
        (0, 10 * 1024 * 1024, 0),
        "prepare",
    )(my_x, tiles, *summed)


def last_kernel(other_ref, back_ref, turned_ref, slope_ref, summed_ref, after_ref, out_ref, total, delta):
    del after_ref
    total[...] = jnp.zeros_like(total)

    def spread(group, carry):
        terms = []
        for k in range(STEP):
            row = group * STEP + k
            rows = pl.ds(pl.multiple_of(row * BS, BS), BS)
            terms.append(jnp.dot(turned_ref[row], back_ref[rows, :], preferred_element_type=F32))
        for k in range(STEP):
            row = group * STEP + k
            total[row] += terms[k][:BS]
            total[other_ref[row]] += terms[k][BS:]
        return carry

    lax.fori_loop(0, NB // STEP, spread, 0)

    def scale(row, carry):
        rows = pl.ds(pl.multiple_of(row * BS, BS), BS)
        delta[rows, :] = (total[row] * slope_ref[rows, :]).astype(BF16)
        return carry

    lax.fori_loop(0, NB, scale, 0, unroll=4)
    out_ref[...] = jnp.dot(summed_ref[...], delta[...], preferred_element_type=F32).astype(BF16)


def last_part(other, back, turned, slope, summed, after):
    return call(
        last_kernel,
        jax.ShapeDtypeStruct((X * BS, BS), BF16),
        [SMEM, VMEM, VMEM, VMEM, VMEM, ANY],
        VMEM,
        [pltpu.VMEM((NB, BS, BS), F32), pltpu.VMEM((ROWS, BS), BF16)],
        (2 * NB * 2 * BS**3 + 2 * ROWS * 512 * BS, 8 * 1024 * 1024, 0),
        "last_part",
    )(other, back, turned, slope, summed, after)


def join_kernel(first_ref, second_ref, after_ref, out_ref):
    del after_ref
    out_ref[:, 0:BS] = first_ref[...]
    out_ref[:, BS:] = second_ref[...]


def join(first, second, after):
    return call(
        join_kernel,
        jax.ShapeDtypeStruct((X * BS, (X + 1) * BS), BF16),
        [VMEM, VMEM, ANY],
        VMEM,
        [],
        (0, 1024 * 1024, 0),
        "join",
    )(first, second, after)


def shift(value, step):
    return lax.ppermute(value, "z", [(i, (i + step) % Z) for i in range(Z)])


def turn(value, step):
    return lax.ppermute(value, "mp", [(i, (i + step) % X) for i in range(X)])


def gather_features(value):
    left, right = turn(value, 1), turn(value, -1)
    half = value.shape[0] // 2
    far = [turn(left[:half], 1), turn(right[half:], -1)]
    return value, left, right, far[0], far[1]


def exchange(value, axes):
    return lax.all_to_all(value, axes, split_axis=0, concat_axis=0, tiled=True)


def plane(staged):
    per = staged.shape[0] // G
    got = exchange(staged.reshape(G, per * BS, BS), ("y", "core"))
    return got.reshape(staged.shape)


def ring(table):
    steps = [(table, table)]
    for _ in range(1, Z // 2):
        up, down = steps[-1]
        steps.append((shift(up, 1), shift(down, -1)))
    up, down = steps[-1]
    return steps, (shift(up[:MIDDLE], 1), shift(down[MIDDLE:], -1))


def body(
    input_history,
    hidden_history,
    batch_blocks,
    tile_columns,
    tile_values,
    send_blocks,
    send_counts,
    weight_first,
    weight_second,
    cotangent,
):
    my_z = lax.axis_index("z").astype(jnp.int32)
    my_x = lax.axis_index("mp").astype(jnp.int32)
    blocks = send_blocks[0].T
    table_input = pack(blocks, send_counts, input_history, tile_columns)
    steps, far = ring(table_input)
    table_hidden = pack(blocks, send_counts, hidden_history, far[0])
    steps_hidden, far_hidden = ring(table_hidden)

    def piece_of(sources, after):
        return plane(stage(my_z.reshape(1), [s if isinstance(s, tuple) else (s,) for s in sources], after))

    halo_input = [
        piece_of(steps[1], tile_columns),
        piece_of((table_input,) + steps[2], tile_columns),
        piece_of((far,) + steps[3], steps_hidden[1][0]),
    ]
    halo_hidden = [
        piece_of(steps_hidden[1], tile_columns),
        piece_of((table_hidden,) + steps_hidden[2], tile_columns),
        piece_of(steps_hidden[3], tile_columns),
        piece_of((far_hidden,), tile_columns),
    ]

    use = tile_columns[:, 2:] - NB
    owner, slot = use // CAP, use % CAP
    group = (owner // (Z * C)) * C + owner % C
    distance = ((owner // C) % Z - my_z) % Z
    near = jnp.minimum(distance, Z - distance)
    from_below = (distance < Z // 2).astype(jnp.int32)
    single = jnp.logical_or(distance == 0, distance == Z // 2)
    third = jnp.where(single, 0, 1 + from_below)
    piece_hidden = jnp.where(near == 0, 1, near - 1)
    piece_input = jnp.minimum(piece_hidden, 2)
    even = group * 2 + from_below
    place_input = jnp.where(near == 1, even, group * 3 + third)
    place_hidden = jnp.where(
        jnp.logical_or(near == 1, near == 3), even, jnp.where(near == Z // 2, group, group * 3 + third)
    )
    where_input = (piece_input.reshape(-1), (place_input * CAP + slot).reshape(-1))
    where_hidden = (piece_hidden.reshape(-1), (place_hidden * CAP + slot).reshape(-1))
    other = tile_columns[:, 1]
    mine = jnp.arange(NB, dtype=jnp.int32)
    local_first = batch_blocks[0][jnp.stack([mine, other], axis=1)].reshape(-1)
    local_second = jnp.stack([mine, other], axis=1).reshape(-1)

    weights = gather_features(jnp.concatenate([weight_first, weight_second]))
    weights = [weights[0], weights[1], weights[2], jnp.concatenate(weights[3:])]
    columns = jnp.concatenate([lax.dynamic_slice(w, (0, my_x * BS), (BS, BS)) for w in weights])
    order = jnp.stack([(-my_x) % X, (1 - my_x) % X, (2 - my_x) % X, (3 - my_x) % X])
    order = jnp.array([0, 2, 3, 1], jnp.int32)[order]
    weight_all = jnp.stack([w[BS:] for w in weights])[order].reshape(X * BS, X * BS)
    cot_rows = exchange(cotangent.reshape(X, QUARTER, BS), "mp")

    summed_first = aggregate(HEAD, table_input, halo_input, tile_values, local_first, *where_input, cot_rows)
    all_first = gather_features(summed_first)
    hidden_first, slope_first = first_layer(all_first, columns)
    turned_tiles, turned_first = prepare(my_x.reshape(1), tile_values, all_first)
    summed_second = aggregate(
        0, hidden_first, halo_hidden, tile_values, local_second, *where_hidden, turned_tiles
    )
    rows_second = exchange(summed_second.reshape(X, QUARTER, BS), "mp")
    out_rows, delta_rows, back_rows = second_layer(rows_second, weight_all, cot_rows)
    back_second = exchange(back_rows, "mp").reshape(ROWS, BS)
    part_second = grad_second_part(rows_second, delta_rows)
    part_first = last_part(other, back_second, turned_tiles, slope_first, turned_first, part_second)
    layer_out = exchange(out_rows, "mp").reshape(ROWS, BS)

    dealt = X * G
    got = join(part_first, part_second, layer_out).reshape(dealt, -1, (X + 1) * BS)
    got = exchange(got, ("mp", "y", "core")).astype(F32)
    got_second = got[:, :, BS:].sum(0)
    got_first = got[:, :, :BS].reshape(X, G, -1, BS).sum(1).transpose(1, 0, 2).reshape(-1, X * BS)
    both = jnp.concatenate([got_first, got_second], axis=0).astype(BF16)
    both = exchange(jnp.broadcast_to(both[None], (Z,) + both.shape), "z").astype(F32).sum(0)
    both = exchange(jnp.broadcast_to(both[None], (G,) + both.shape), ("y", "core"))
    both = both.reshape(G, 2, -1, X * BS)
    grad_first = both[:, 0].reshape(BS, X * BS)
    grad_second = both[:, 1].reshape(BS, X * BS)
    return (layer_out, grad_first, grad_second)


def solution(mesh):
    inner = Mesh(mesh.devices.reshape(Y, Z, C, X), ("y", "z", "core", "mp"))
    nodes = ("y", "z", "core")
    placed = (
        P(nodes, "mp"),
        P(nodes, "mp"),
        P(nodes, None),
        P(nodes, None),
        P(nodes, None, None, None),
        P(nodes, None, None),
        P(nodes, None),
        P("mp", None),
        P("mp", None),
        P(nodes, "mp"),
    )
    return jax.shard_map(
        body,
        mesh=inner,
        in_specs=placed,
        out_specs=(P(nodes, "mp"), P("mp", None), P("mp", None)),
        check_vma=False,
    )
```

```python
import functools

import jax
import jax.numpy as jnp
from jax import lax
from jax.experimental import pallas as pl
from jax.experimental.pallas import tpu as pltpu
from jax.sharding import Mesh
from jax.sharding import PartitionSpec as P

Y, Z, C, X = 4, 8, 2, 4
G = Y * C
BS = 128
NB = 24
TPR = 5
CAP = 3
HB = 32
ROWS = NB * BS
QUARTER = ROWS // X
STEP = 4
F32 = jnp.float32
BF16 = jnp.bfloat16
ANY = pl.BlockSpec(memory_space=pltpu.HBM)
VMEM = pl.BlockSpec(memory_space=pltpu.VMEM)
SMEM = pl.BlockSpec(memory_space=pltpu.SMEM)
LIMIT = 48 * 1024 * 1024


def call(kernel, out_shape, in_specs, out_specs, scratch, cost, name):
    return pl.pallas_call(
        kernel,
        out_shape=out_shape,
        in_specs=in_specs,
        out_specs=out_specs,
        scratch_shapes=scratch,
        compiler_params=pltpu.CompilerParams(vmem_limit_bytes=LIMIT),
        cost_estimate=pl.CostEstimate(flops=cost[0], bytes_accessed=cost[1], transcendentals=cost[2]),
        name=name,
    )


HEAD = 16
HALF = HB // 2
MIDDLE = HEAD + HALF * BS


def pack_kernel(blocks_ref, counts_ref, history_ref, after_ref, out_ref, wanted):
    del after_ref
    wanted[...] = jnp.zeros_like(wanted)
    blocks = blocks_ref[...]
    slot = lax.broadcasted_iota(jnp.int32, blocks.shape, 0)
    wanted[0:CAP, 0 : blocks.shape[1]] = jnp.where(slot < counts_ref[...], blocks, HB)
    out_ref[0:HEAD, :] = wanted[...].astype(F32).astype(BF16)

    def one(block, carry):
        rows = pl.multiple_of(block * BS, BS)
        out_ref[pl.ds(pl.multiple_of(HEAD + rows, HEAD), BS), :] = history_ref[pl.ds(rows, BS), :].astype(BF16)
        return carry

    lax.fori_loop(0, HB, one, 0)


def pack(blocks, counts, history, after):
    return call(
        pack_kernel,
        jax.ShapeDtypeStruct((HEAD + HB * BS, BS), BF16),
        [VMEM, VMEM, VMEM, ANY],
        VMEM,
        [pltpu.VMEM((HEAD, BS), jnp.int32)],
        (0, 3 * 1024 * 1024, 0),
        "pack",
    )(blocks, counts, history, after)


def stage_kernel(sizes, z_ref, *refs):
    count = len(sizes)
    total = sum(sizes)
    flat, (out_ref, ints, asked, sem) = refs[:total], refs[-4:]
    sources = [flat[sum(sizes[:s]) : sum(sizes[: s + 1])] for s in range(count)]
    copies = [pltpu.make_async_copy(ints.at[s], asked.at[s], sem.at[s]) for s in range(count)]
    for s in range(count):
        ints[s] = sources[s][0][0:HEAD, :].astype(F32).astype(jnp.int32)
        copies[s].start()
    for copy in copies:
        copy.wait()
    mine = z_ref[0]
    zeros = jnp.zeros((BS, BS), BF16)

    def one(reader, carry):
        column = (reader // C) * (Z * C) + mine * C + lax.rem(reader, C)
        for s, source in enumerate(sources):
            for slot in range(CAP):
                block = asked[s, slot, column]
                entry = (reader * count + s) * CAP + slot
                if len(source) == 1:
                    start = pl.multiple_of(HEAD + jnp.minimum(block, HB - 1) * BS, HEAD)
                    out_ref[entry] = jnp.where(block < HB, source[0][pl.ds(start, BS), :], zeros)
                else:
                    first = pl.multiple_of(HEAD + jnp.minimum(block, HALF - 1) * BS, HEAD)
                    second = pl.multiple_of(jnp.clip(block - HALF, 0, HALF - 1) * BS, BS)
                    late = jnp.where(block < HB, source[1][pl.ds(second, BS), :], zeros)
                    out_ref[entry] = jnp.where(block < HALF, source[0][pl.ds(first, BS), :], late)
        return carry

    lax.fori_loop(0, G, one, 0)


def stage(my_z, sources, after=()):
    count = len(sources)
    sizes = tuple(len(source) for source in sources)
    entries = G * CAP * count
    return call(
        functools.partial(stage_kernel, sizes),
        jax.ShapeDtypeStruct((entries, BS, BS), BF16),
        [SMEM] + [VMEM] * sum(sizes) + [ANY] * len(after),
        VMEM,
        [
            pltpu.VMEM((count, HEAD, BS), jnp.int32),
            pltpu.SMEM((count, HEAD, BS), jnp.int32),
            pltpu.SemaphoreType.DMA((count,)),
        ],
        (0, 2 * entries * BS * BS * 2, 0),
        "stage",
    )(my_z, *[part for source in sources for part in source], *after)


def aggregate_kernel(sides, count, skip, code_ref, other_ref, blocks_ref, table_ref, *refs):
    halos, refs = refs[:count], refs[count:]
    tiles_ref, out_ref, table, halo, tiles, table_sem, halo_sem, tiles_sem = refs

    def local(row):
        pair = (row, other_ref[row])
        return [blocks_ref[block] for block in pair] if skip else pair

    copy = pltpu.make_async_copy(table_ref.at[pl.ds(skip, table.shape[0])], table, table_sem)
    copy.start()

    def start(row, carry):
        pltpu.make_async_copy(tiles_ref.at[row], tiles.at[row], tiles_sem.at[row // STEP]).start()
        for slot in range(TPR - 2):
            code = code_ref[row * (TPR - 2) + slot]
            distance, group, number = code // 256, lax.rem(code // 8, 32), lax.rem(code, 8)
            for side, (piece, source, sources) in enumerate(sides):

                @pl.when(distance == side)
                def _(piece=piece, source=source, sources=sources, group=group, number=number, slot=slot):
                    place = (group * sources + source) * CAP + number
                    pltpu.make_async_copy(halos[piece].at[place], halo.at[row, slot], halo_sem.at[row // STEP]).start()

        return carry

    lax.fori_loop(0, NB, start, 0)
    copy.wait()

    def compute(group, carry):
        rows = pl.ds(group * STEP, STEP)
        pltpu.make_async_copy(tiles_ref.at[rows], tiles.at[rows], tiles_sem.at[group]).wait()
        pltpu.make_async_copy(halo.at[rows], halo.at[rows], halo_sem.at[group]).wait()
        for k in range(STEP):
            row = group * STEP + k
            left = jnp.concatenate([tiles[row, t] for t in range(TPR)], axis=1)
            right = jnp.concatenate(
                [table[pl.ds(pl.multiple_of(block * BS, BS), BS), :] for block in local(row)]
                + [halo[row, t] for t in range(TPR - 2)],
                axis=0,
            )
            summed = jnp.dot(left, right, preferred_element_type=F32)
            out_ref[pl.ds(pl.multiple_of(row * BS, BS), BS), :] = summed.astype(BF16)
        return carry

    lax.fori_loop(0, NB // STEP, compute, 0)


def aggregate(sides, skip, table, halos, tiles, code, other, blocks):
    return call(
        functools.partial(aggregate_kernel, sides, len(halos), skip),
        jax.ShapeDtypeStruct((ROWS, BS), BF16),
        [SMEM] * 3 + [ANY] * (len(halos) + 2),
        VMEM,
        [
            pltpu.VMEM((table.shape[0] - skip, BS), BF16),
            pltpu.VMEM((NB, TPR - 2, BS, BS), BF16),
            pltpu.VMEM((NB, TPR, BS, BS), BF16),
            pltpu.SemaphoreType.DMA,
            pltpu.SemaphoreType.DMA((NB // STEP,)),
            pltpu.SemaphoreType.DMA((NB // STEP,)),
        ],
        (2 * NB * TPR * BS**3, 2 * NB * TPR * BS * BS * 2, 0),
        "aggregate",
    )(code, other, blocks, table, *halos, tiles)


def sigmoid(value):
    return 1.0 / (1.0 + jnp.exp(-value))


def first_kernel(s0, s1, s2, far0, far1, weight_ref, hidden_ref, slope_ref):
    weight = weight_ref[...]
    step = 256
    half = ROWS // 2 // step

    def one(far, begin, row, carry):
        rows = pl.ds(pl.multiple_of((row + begin) * step, step), step)
        far_rows = pl.ds(pl.multiple_of(row * step, step), step)
        left = jnp.concatenate([s0[rows, :], s1[rows, :], s2[rows, :], far[far_rows, :]], axis=1)
        pre = jnp.dot(left, weight, preferred_element_type=F32)
        sig = sigmoid(pre)
        hidden_ref[rows, :] = (pre * sig).astype(BF16)
        slope_ref[rows, :] = sig * (1.0 + pre * (1.0 - sig))
        return carry

    lax.fori_loop(0, half, functools.partial(one, far0, 0), 0)
    lax.fori_loop(0, half, functools.partial(one, far1, half), 0)


def first_layer(summed, weight):
    return call(
        first_kernel,
        (jax.ShapeDtypeStruct((ROWS, BS), BF16), jax.ShapeDtypeStruct((ROWS, BS), F32)),
        [VMEM] * 6,
        (VMEM, VMEM),
        [],
        (2 * ROWS * 512 * BS, 6 * 1024 * 1024, ROWS * BS),
        "first_layer",
    )(*summed, weight)


def second_kernel(x_ref, summed_ref, weight_ref, cot_ref, out_ref, delta_ref, back_ref):
    step = 128

    def one(row, carry):
        rows = pl.ds(pl.multiple_of(row * step, step), step)
        left = jnp.concatenate([summed_ref[k, rows, :] for k in range(X)], axis=1)
        cot = jnp.concatenate([cot_ref[k, rows, :] for k in range(X)], axis=1)
        pre = jnp.dot(left, weight_ref[...], preferred_element_type=F32)
        sig = sigmoid(pre)
        out = (pre * sig).astype(BF16)
        delta = (cot.astype(F32) * (sig * (1.0 + pre * (1.0 - sig)))).astype(BF16)
        back = lax.dot_general(
            delta, weight_ref[...], (((1,), (1,)), ((), ())), preferred_element_type=F32
        ).astype(BF16)
        delta_ref[rows, :] = delta
        for k in range(X):
            out_ref[lax.rem(k + X - x_ref[0], X), rows, :] = out[:, k * BS : (k + 1) * BS]
            back_ref[k, rows, :] = back[:, k * BS : (k + 1) * BS]
        return carry

    lax.fori_loop(0, QUARTER // step, one, 0)


def second_layer(my_x, summed, weight, cot):
    piece = jax.ShapeDtypeStruct((X, QUARTER, BS), BF16)
    return call(
        second_kernel,
        (piece, jax.ShapeDtypeStruct((QUARTER, X * BS), BF16), piece),
        [SMEM] + [VMEM] * 3,
        (VMEM,) * 3,
        [],
        (4 * QUARTER * 512 * 512, 5 * 1024 * 1024, QUARTER * 512),
        "second_layer",
    )(my_x, summed, weight, cot)


def grad_second_kernel(summed_ref, delta_ref, out_ref):
    for k in range(X):
        out_ref[k * BS : (k + 1) * BS, :] = lax.dot_general(
            summed_ref[k], delta_ref[...], (((0,), (0,)), ((), ())), preferred_element_type=F32
        ).astype(BF16)


def grad_second_part(summed, delta):
    return call(
        grad_second_kernel,
        jax.ShapeDtypeStruct((X * BS, X * BS), BF16),
        [VMEM] * 2,
        VMEM,
        [],
        (2 * QUARTER * 512 * 512, 3 * 1024 * 1024, 0),
        "grad_second",
    )(summed, delta)


def prepare_kernel(x_ref, tiles_ref, s0, s1, s2, far0, far1, turned_ref, summed_ref, tiles, sem):
    def start(row, carry):
        pltpu.make_async_copy(tiles_ref.at[row, pl.ds(0, 2)], tiles.at[row], sem).start()
        return carry

    lax.fori_loop(0, NB, start, 0)
    x = x_ref[0]
    half = ROWS // 2
    for source, step, begin in ((s0, 0, 0), (s1, X - 1, 0), (s2, 1, 0), (far0, 2, 0), (far1, 2, half)):
        place = pl.ds(pl.multiple_of(lax.rem(x + step, X) * BS, BS), BS)

        def one(block, carry, source=source, begin=begin, place=place):
            rows = pl.ds(pl.multiple_of(block * BS, BS), BS)
            columns = pl.ds(pl.multiple_of(begin + block * BS, BS), BS)
            summed_ref[place, columns] = source[rows, :].T
            return carry

        lax.fori_loop(0, source.shape[0] // BS, one, 0, unroll=4)
    pltpu.make_async_copy(tiles, tiles, sem).wait()

    def turn_tiles(row, carry):
        for t in range(2):
            turned_ref[row, pl.ds(t * BS, BS), :] = tiles[row, t].T
        return carry

    lax.fori_loop(0, NB, turn_tiles, 0, unroll=2)


def prepare(my_x, tiles, summed):
    return call(
        prepare_kernel,
        (jax.ShapeDtypeStruct((NB, 2 * BS, BS), BF16), jax.ShapeDtypeStruct((X * BS, ROWS), BF16)),
        [SMEM, ANY] + [VMEM] * 5,
        (VMEM, VMEM),
        [pltpu.VMEM((NB, 2, BS, BS), BF16), pltpu.SemaphoreType.DMA],
        (0, 10 * 1024 * 1024, 0),
        "prepare",
    )(my_x, tiles, *summed)


def last_kernel(other_ref, back_ref, turned_ref, slope_ref, summed_ref, second_ref, out_ref, total, delta):
    out_ref[:, BS:] = second_ref[...]
    total[...] = jnp.zeros_like(total)

    def spread(group, carry):
        terms = []
        for k in range(STEP):
            row = group * STEP + k
            rows = pl.ds(pl.multiple_of(row * BS, BS), BS)
            terms.append(jnp.dot(turned_ref[row], back_ref[rows, :], preferred_element_type=F32))
        for k in range(STEP):
            row = group * STEP + k
            total[row] += terms[k][:BS]
            total[other_ref[row]] += terms[k][BS:]
        return carry

    lax.fori_loop(0, NB // STEP, spread, 0)

    def scale(row, carry):
        rows = pl.ds(pl.multiple_of(row * BS, BS), BS)
        delta[rows, :] = (total[row] * slope_ref[rows, :]).astype(BF16)
        return carry

    lax.fori_loop(0, NB, scale, 0, unroll=4)
    out_ref[:, 0:BS] = jnp.dot(summed_ref[...], delta[...], preferred_element_type=F32).astype(BF16)


def last_part(other, back, turned, slope, summed, second):
    return call(
        last_kernel,
        jax.ShapeDtypeStruct((X * BS, (X + 1) * BS), BF16),
        [SMEM] + [VMEM] * 5,
        VMEM,
        [pltpu.VMEM((NB, BS, BS), F32), pltpu.VMEM((ROWS, BS), BF16)],
        (2 * NB * 2 * BS**3 + 2 * ROWS * 512 * BS, 8 * 1024 * 1024, 0),
        "last_part",
    )(other, back, turned, slope, summed, second)


def sum_kernel(got_ref, held_ref, out_ref, passed_ref):
    del held_ref, passed_ref
    rows = got_ref.shape[1]
    second = got_ref[0, :, BS:].astype(F32)
    for k in range(1, X * G):
        second += got_ref[k, :, BS:].astype(F32)
    for x in range(X):
        first = got_ref[x * G, :, :BS].astype(F32)
        for k in range(1, G):
            first += got_ref[x * G + k, :, :BS].astype(F32)
        for z in range(Z):
            out_ref[z, :rows, x * BS : (x + 1) * BS] = first.astype(BF16)
    for z in range(Z):
        out_ref[z, rows:, :] = second.astype(BF16)


def sum_parts(got, held):
    return pl.pallas_call(
        sum_kernel,
        out_shape=(
            jax.ShapeDtypeStruct((Z, 2 * got.shape[1], X * BS), BF16),
            jax.ShapeDtypeStruct(held.shape, held.dtype),
        ),
        in_specs=[VMEM, ANY],
        out_specs=(VMEM, ANY),
        input_output_aliases={1: 1},
        compiler_params=pltpu.CompilerParams(vmem_limit_bytes=LIMIT),
        cost_estimate=pl.CostEstimate(flops=0, bytes_accessed=1024 * 1024, transcendentals=0),
        name="sum_parts",
    )(got, held)


def assemble_kernel(x_ref, *refs):
    quarters, (out_ref, sem) = refs[:X], refs[X:]
    for k in range(X):
        rows = pl.ds(pl.multiple_of(lax.rem(x_ref[0] + X - k, X) * QUARTER, QUARTER), QUARTER)
        pltpu.make_async_copy(quarters[k], out_ref.at[rows], sem).start()
    pltpu.make_async_copy(out_ref, out_ref, sem).wait()


def assemble(my_x, quarters):
    return call(
        assemble_kernel,
        jax.ShapeDtypeStruct((ROWS, BS), BF16),
        [SMEM] + [VMEM] * X,
        ANY,
        [pltpu.SemaphoreType.DMA],
        (0, 2 * 1024 * 1024, 0),
        "assemble",
    )(my_x, *quarters)


def shift(value, step):
    return lax.ppermute(value, "z", [(i, (i + step) % Z) for i in range(Z)])


def turn(value, step):
    return lax.ppermute(value, "mp", [(i, (i + step) % X) for i in range(X)])


def gather_features(value):
    left, right = turn(value, 1), turn(value, -1)
    half = value.shape[0] // 2
    far = [turn(left[:half], 1), turn(right[half:], -1)]
    return value, left, right, far[0], far[1]


def exchange(value, axes):
    return lax.all_to_all(value, axes, split_axis=0, concat_axis=0, tiled=True)


def plane(staged):
    per = staged.shape[0] // G
    got = exchange(staged.reshape(G, per * BS, BS), ("y", "core"))
    return got.reshape(staged.shape)


def apart(work, my_z, *args):
    def skip(*args):
        return jax.tree.map(lambda leaf: jnp.zeros(leaf.shape, leaf.dtype), shapes)

    shapes = jax.eval_shape(work, *args)
    return lax.cond(my_z < Z, work, skip, *args)


def body(
    input_history,
    hidden_history,
    batch_blocks,
    tile_columns,
    tile_values,
    send_blocks,
    send_counts,
    weight_first,
    weight_second,
    cotangent,
):
    my_z = lax.axis_index("z").astype(jnp.int32)
    my_x = lax.axis_index("mp").astype(jnp.int32)
    blocks = send_blocks[0].T
    other = tile_columns[:, 1]
    table_input = pack(blocks, send_counts, input_history, tile_columns)

    def hop(pair):
        return shift(pair[0], 1), shift(pair[1], -1)

    def far_hop(pair):
        return shift(pair[0][:MIDDLE], 1), shift(pair[1][MIDDLE:], -1)

    def send(*sources, after=()):
        return plane(stage(my_z.reshape(1), [s if isinstance(s, tuple) else (s,) for s in sources], after))

    def beside(*sources, after=()):
        return apart(lambda sources, after: send(*sources, after=after), my_z, sources, after)

    def step_zero(table, blocks, counts, history):
        return hop((table, table)), beside(table), pack(blocks, counts, history, table)

    def step_one(pair, other):
        return hop(pair), hop((other, other)), beside(*pair, other)

    def step_two(pair, other):
        return hop(pair), hop(other), beside(*pair, *other)

    def step_three(pair, other):
        return far_hop(pair), hop(other), beside(*pair, other[0])

    def step_four(far, other, after):
        return far_hop(other), beside(far, after=after)

    weights = lax.all_gather(jnp.concatenate([weight_first, weight_second]), "mp", axis=0, tiled=False)
    cot = lax.all_gather(cotangent, "mp", axis=0, tiled=False)
    cot_rows = lax.dynamic_slice(cot, (0, my_x * QUARTER, 0), (X, QUARTER, BS))
    order = jnp.stack([my_x, (my_x - 1) % X, (my_x + 1) % X, (my_x + 2) % X])
    columns = lax.dynamic_slice(weights, (0, 0, my_x * BS), (X, BS, BS))[order].reshape(X * BS, BS)
    weight_all = weights[:, BS:].reshape(X * BS, X * BS)

    one, piece0, table_hidden = apart(step_zero, my_z, table_input, blocks, send_counts, hidden_history)
    two, one_hidden, piece1 = apart(step_one, my_z, one, table_hidden)
    three, two_hidden, piece2 = apart(step_two, my_z, two, one_hidden)
    far, three_hidden, piece3 = apart(step_three, my_z, three, two_hidden)
    far_hidden, piece4 = apart(step_four, my_z, far, three_hidden, (columns, weight_all, cot_rows))
    piece5 = send(far_hidden, *three_hidden, two_hidden[1])

    sides_input = ((0, 0, 1), (1, 1, 3), (2, 1, 4), (3, 1, 3), (4, 0, 1), (3, 0, 3), (2, 0, 4), (1, 0, 3))
    sides_hidden = ((0, 2, 3), (1, 3, 4), (3, 3, 4), (3, 2, 4), (3, 0, 4), (3, 1, 4), (2, 2, 3), (1, 2, 4))
    use = tile_columns[:, 2:] - NB
    owner, slot = use // CAP, use % CAP
    group = (owner // (Z * C)) * C + owner % C
    code = (((owner // C) % Z - my_z) % Z * 256 + group * 8 + slot).reshape(-1)

    batch = batch_blocks.reshape(-1)
    halo_input = (piece0, piece1, piece2, piece3, piece4)
    halo_hidden = (piece1, piece2, piece3, piece5)
    summed_first = aggregate(sides_input, HEAD, table_input, halo_input, tile_values, code, other, batch)
    all_first = gather_features(summed_first)
    hidden_first, slope_first = first_layer(all_first, columns)
    turned_tiles, turned_first = prepare(my_x.reshape(1), tile_values, all_first)
    summed_second = aggregate(sides_hidden, 0, hidden_first, halo_hidden, tile_values, code, other, batch)
    rows_second = exchange(summed_second.reshape(X, QUARTER, BS), "mp")
    out_rows, delta_rows, back_rows = second_layer(
        my_x.reshape(1), rows_second, weight_all, cot_rows
    )
    back_second = exchange(back_rows, "mp").reshape(ROWS, BS)
    part_second = grad_second_part(rows_second, delta_rows)
    got = last_part(other, back_second, turned_tiles, slope_first, turned_first, part_second)

    dealt = X * G
    got = exchange(got.reshape(dealt, -1, (X + 1) * BS), ("mp", "y", "core"))
    parts, out_rows = sum_parts(got, out_rows)
    quarters = [out_rows[0]] + [turn(out_rows[k], k) for k in range(1, X)]
    layer_out = assemble(my_x.reshape(1), quarters)
    both = exchange(parts, "z").astype(F32).sum(0).astype(BF16)
    both = exchange(jnp.broadcast_to(both[None], (G,) + both.shape), ("y", "core"))
    both = both.reshape(G, 2, -1, X * BS).astype(F32)
    grad_first = both[:, 0].reshape(BS, X * BS)
    grad_second = both[:, 1].reshape(BS, X * BS)
    return (layer_out, grad_first, grad_second)


def solution(mesh):
    inner = Mesh(mesh.devices.reshape(Y, Z, C, X), ("y", "z", "core", "mp"))
    nodes = ("y", "z", "core")
    placed = (
        P(nodes, "mp"),
        P(nodes, "mp"),
        P(nodes, None),
        P(nodes, None),
        P(nodes, None, None, None),
        P(nodes, None, None),
        P(nodes, None),
        P("mp", None),
        P("mp", None),
        P(nodes, "mp"),
    )
    return jax.shard_map(
        body,
        mesh=inner,
        in_specs=placed,
        out_specs=(P(nodes, "mp"), P("mp", None), P("mp", None)),
        check_vma=False,
    )
```

```python
import functools

import jax
import jax.numpy as jnp
from jax import lax
from jax.experimental import pallas as pl
from jax.experimental.pallas import tpu as pltpu
from jax.sharding import Mesh
from jax.sharding import PartitionSpec as P

Y, Z, C, X = 4, 8, 2, 4
G = Y * C
BS = 128
NB = 24
TPR = 5
CAP = 3
HB = 32
ROWS = NB * BS
QUARTER = ROWS // X
STEP = 4
F32 = jnp.float32
BF16 = jnp.bfloat16
ANY = pl.BlockSpec(memory_space=pltpu.HBM)
VMEM = pl.BlockSpec(memory_space=pltpu.VMEM)
SMEM = pl.BlockSpec(memory_space=pltpu.SMEM)
LIMIT = 48 * 1024 * 1024


def call(kernel, out_shape, in_specs, out_specs, scratch, cost, name):
    return pl.pallas_call(
        kernel,
        out_shape=out_shape,
        in_specs=in_specs,
        out_specs=out_specs,
        scratch_shapes=scratch,
        compiler_params=pltpu.CompilerParams(vmem_limit_bytes=LIMIT),
        cost_estimate=pl.CostEstimate(flops=cost[0], bytes_accessed=cost[1], transcendentals=cost[2]),
        name=name,
    )


HEAD = 16
HALF = HB // 2
MIDDLE = HEAD + HALF * BS


def pack_kernel(blocks_ref, counts_ref, history_ref, out_ref, wanted, rows_in, sem):
    parts = sem.shape[0]
    size = HB * BS // parts
    copies = [
        pltpu.make_async_copy(history_ref.at[pl.ds(k * size, size)], rows_in.at[pl.ds(k * size, size)], sem.at[k])
        for k in range(parts)
    ]
    for copy in copies:
        copy.start()
    wanted[...] = jnp.zeros_like(wanted)
    blocks = blocks_ref[...]
    slot = lax.broadcasted_iota(jnp.int32, blocks.shape, 0)
    wanted[0:CAP, 0 : blocks.shape[1]] = jnp.where(slot < counts_ref[...], blocks, HB)
    out_ref[0:HEAD, :] = wanted[...].astype(F32).astype(BF16)
    for k in range(parts):
        copies[k].wait()

        def one(block, carry, k=k):
            rows = pl.multiple_of(k * size + block * BS, BS)
            out_ref[pl.ds(pl.multiple_of(HEAD + rows, HEAD), BS), :] = rows_in[pl.ds(rows, BS), :].astype(BF16)
            return carry

        lax.fori_loop(0, size // BS, one, 0, unroll=2)


def pack(blocks, counts, history):
    return call(
        pack_kernel,
        jax.ShapeDtypeStruct((HEAD + HB * BS, BS), BF16),
        [VMEM, VMEM, ANY],
        VMEM,
        [
            pltpu.VMEM((HEAD, BS), jnp.int32),
            pltpu.VMEM(history.shape, F32),
            pltpu.SemaphoreType.DMA((4,)),
        ],
        (0, 3 * 1024 * 1024, 0),
        "pack",
    )(blocks, counts, history)


def stage_kernel(sizes, z_ref, *refs):
    count = len(sizes)
    total = sum(sizes)
    flat, (out_ref, ints, asked, sem) = refs[:total], refs[-4:]
    sources = [flat[sum(sizes[:s]) : sum(sizes[: s + 1])] for s in range(count)]
    copies = [pltpu.make_async_copy(ints.at[s], asked.at[s], sem.at[s]) for s in range(count)]
    for s in range(count):
        ints[s] = sources[s][0][0:HEAD, :].astype(F32).astype(jnp.int32)
        copies[s].start()
    for copy in copies:
        copy.wait()
    mine = z_ref[0]
    zeros = jnp.zeros((BS, BS), BF16)

    def block_of(source, block):
        if len(source) == 1:
            start = pl.multiple_of(HEAD + jnp.minimum(block, HB - 1) * BS, HEAD)
            return jnp.where(block < HB, source[0][pl.ds(start, BS), :], zeros)
        first = pl.multiple_of(HEAD + jnp.minimum(block, HALF - 1) * BS, HEAD)
        second = pl.multiple_of(jnp.clip(block - HALF, 0, HALF - 1) * BS, BS)
        late = jnp.where(block < HB, source[1][pl.ds(second, BS), :], zeros)
        return jnp.where(block < HALF, source[0][pl.ds(first, BS), :], late)

    def one(reader, carry):
        column = (reader // C) * (Z * C) + mine * C + lax.rem(reader, C)
        for s, source in enumerate(sources):
            found = [block_of(source, asked[s, slot, column]) for slot in range(CAP)]
            for slot in range(CAP):
                out_ref[(reader * count + s) * CAP + slot] = found[slot]
        return carry

    lax.fori_loop(0, G, one, 0)


def stage(my_z, sources, after=()):
    count = len(sources)
    sizes = tuple(len(source) for source in sources)
    entries = G * CAP * count
    return call(
        functools.partial(stage_kernel, sizes),
        jax.ShapeDtypeStruct((entries, BS, BS), BF16),
        [SMEM] + [VMEM] * sum(sizes) + [ANY] * len(after),
        VMEM,
        [
            pltpu.VMEM((count, HEAD, BS), jnp.int32),
            pltpu.SMEM((count, HEAD, BS), jnp.int32),
            pltpu.SemaphoreType.DMA((count,)),
        ],
        (0, 2 * entries * BS * BS * 2, 0),
        "stage",
    )(my_z, *[part for source in sources for part in source], *after)


def aggregate_kernel(sides, count, skip, code_ref, other_ref, blocks_ref, table, tiles, *refs):
    halos, (out_ref, halo, sem) = refs[:count], refs[count:]

    def local(row):
        pair = (row, other_ref[row])
        return [blocks_ref[block] for block in pair] if skip else pair

    def start(row, carry):
        for slot in range(TPR - 2):
            code = code_ref[row * (TPR - 2) + slot]
            distance, group, number = code >> 8, (code >> 3) & 31, code & 7
            for side, (piece, source, sources) in enumerate(sides):

                @pl.when(distance == side)
                def _(piece=piece, source=source, sources=sources, group=group, number=number, slot=slot):
                    place = (group * sources + source) * CAP + number
                    pltpu.make_async_copy(halos[piece].at[place], halo.at[row, slot], sem.at[row >> 2]).start()

        return carry

    lax.fori_loop(0, NB, start, 0)

    def compute(group, carry):
        rows = pl.ds(group * STEP, STEP)
        pltpu.make_async_copy(halo.at[rows], halo.at[rows], sem.at[group]).wait()
        for k in range(STEP):
            row = group * STEP + k
            left = jnp.concatenate([tiles[row, t] for t in range(TPR)], axis=1)
            right = jnp.concatenate(
                [table[pl.ds(pl.multiple_of(skip + block * BS, HEAD), BS), :] for block in local(row)]
                + [halo[row, t] for t in range(TPR - 2)],
                axis=0,
            )
            summed = jnp.dot(left, right, preferred_element_type=F32)
            out_ref[pl.ds(pl.multiple_of(row * BS, BS), BS), :] = summed.astype(BF16)
        return carry

    lax.fori_loop(0, NB // STEP, compute, 0)


def aggregate(sides, skip, table, halos, tiles, code, other, blocks):
    return call(
        functools.partial(aggregate_kernel, sides, len(halos), skip),
        jax.ShapeDtypeStruct((ROWS, BS), BF16),
        [SMEM] * 3 + [VMEM] * 2 + [ANY] * len(halos),
        VMEM,
        [pltpu.VMEM((NB, TPR - 2, BS, BS), BF16), pltpu.SemaphoreType.DMA((NB // STEP,))],
        (2 * NB * TPR * BS**3, 2 * NB * TPR * BS * BS * 2, 0),
        "aggregate",
    )(code, other, blocks, table, tiles, *halos)


def sigmoid(value):
    return 1.0 / (1.0 + jnp.exp(-value))


def first_kernel(s0, s1, s2, far0, far1, weight_ref, hidden_ref, slope_ref):
    weight = weight_ref[...]
    step = 256
    half = ROWS // 2 // step

    def one(far, begin, row, carry):
        rows = pl.ds(pl.multiple_of((row + begin) * step, step), step)
        far_rows = pl.ds(pl.multiple_of(row * step, step), step)
        left = jnp.concatenate([s0[rows, :], s1[rows, :], s2[rows, :], far[far_rows, :]], axis=1)
        pre = jnp.dot(left, weight, preferred_element_type=F32)
        sig = sigmoid(pre)
        hidden_ref[rows, :] = (pre * sig).astype(BF16)
        slope_ref[rows, :] = sig * (1.0 + pre * (1.0 - sig))
        return carry

    lax.fori_loop(0, half, functools.partial(one, far0, 0), 0)
    lax.fori_loop(0, half, functools.partial(one, far1, half), 0)


def first_layer(summed, weight):
    return call(
        first_kernel,
        (jax.ShapeDtypeStruct((ROWS, BS), BF16), jax.ShapeDtypeStruct((ROWS, BS), F32)),
        [VMEM] * 6,
        (VMEM, VMEM),
        [],
        (2 * ROWS * 512 * BS, 6 * 1024 * 1024, ROWS * BS),
        "first_layer",
    )(*summed, weight)


def second_kernel(x_ref, summed_ref, weight_ref, cot_ref, after_ref, out_ref, grad_ref, back_ref, delta_ref):
    del after_ref
    step = 128

    def one(row, carry):
        rows = pl.ds(pl.multiple_of(row * step, step), step)
        left = jnp.concatenate([summed_ref[k, rows, :] for k in range(X)], axis=1)
        cot = jnp.concatenate([cot_ref[k, rows, :] for k in range(X)], axis=1)
        pre = jnp.dot(left, weight_ref[...], preferred_element_type=F32)
        sig = sigmoid(pre)
        out = (pre * sig).astype(BF16)
        delta = (cot.astype(F32) * (sig * (1.0 + pre * (1.0 - sig)))).astype(BF16)
        back = lax.dot_general(
            delta, weight_ref[...], (((1,), (1,)), ((), ())), preferred_element_type=F32
        ).astype(BF16)
        delta_ref[rows, :] = delta
        for k in range(X):
            out_ref[lax.rem(k + X - x_ref[0], X), rows, :] = out[:, k * BS : (k + 1) * BS]
            back_ref[k, rows, :] = back[:, k * BS : (k + 1) * BS]
        return carry

    lax.fori_loop(0, QUARTER // step, one, 0)
    for k in range(X):
        grad_ref[k * BS : (k + 1) * BS, :] = lax.dot_general(
            summed_ref[k], delta_ref[...], (((0,), (0,)), ((), ())), preferred_element_type=F32
        ).astype(BF16)


def second_layer(my_x, summed, weight, cot, after):
    piece = jax.ShapeDtypeStruct((X, QUARTER, BS), BF16)
    return call(
        second_kernel,
        (piece, jax.ShapeDtypeStruct((X * BS, X * BS), BF16), piece),
        [SMEM] + [VMEM] * 3 + [ANY],
        (VMEM,) * 3,
        [pltpu.VMEM((QUARTER, X * BS), BF16)],
        (6 * QUARTER * 512 * 512, 5 * 1024 * 1024, QUARTER * 512),
        "second_layer",
    )(my_x, summed, weight, cot, after)


def turn_kernel(tiles_ref, after_ref, turned_ref, tiles, sem):
    del after_ref

    def start(row, carry):
        pltpu.make_async_copy(tiles_ref.at[row, pl.ds(0, 2)], tiles.at[row], sem).start()
        return carry

    lax.fori_loop(0, NB, start, 0)
    pltpu.make_async_copy(tiles, tiles, sem).wait()

    def turn_tiles(row, carry):
        for t in range(2):
            turned_ref[row, pl.ds(t * BS, BS), :] = tiles[row, t].T
        return carry

    lax.fori_loop(0, NB, turn_tiles, 0, unroll=2)


def turn_local(tiles, after):
    return call(
        turn_kernel,
        jax.ShapeDtypeStruct((NB, 2 * BS, BS), BF16),
        [ANY, ANY],
        VMEM,
        [pltpu.VMEM((NB, 2, BS, BS), BF16), pltpu.SemaphoreType.DMA],
        (0, 4 * 1024 * 1024, 0),
        "turn_local",
    )(tiles, after)


def prepare_kernel(x_ref, s0, s1, s2, far0, far1, summed_ref):
    x = x_ref[0]
    half = ROWS // 2
    for source, step, begin in ((s0, 0, 0), (s1, X - 1, 0), (s2, 1, 0), (far0, 2, 0), (far1, 2, half)):
        place = pl.ds(pl.multiple_of(lax.rem(x + step, X) * BS, BS), BS)

        def one(block, carry, source=source, begin=begin, place=place):
            rows = pl.ds(pl.multiple_of(block * BS, BS), BS)
            columns = pl.ds(pl.multiple_of(begin + block * BS, BS), BS)
            summed_ref[place, columns] = source[rows, :].T
            return carry

        lax.fori_loop(0, source.shape[0] // BS, one, 0, unroll=4)


def prepare(my_x, summed):
    return call(
        prepare_kernel,
        jax.ShapeDtypeStruct((X * BS, ROWS), BF16),
        [SMEM] + [VMEM] * 5,
        VMEM,
        [],
        (0, 7 * 1024 * 1024, 0),
        "prepare",
    )(my_x, *summed)


def last_kernel(other_ref, back_ref, turned_ref, slope_ref, summed_ref, second_ref, out_ref, total, delta):
    out_ref[:, BS:] = second_ref[...]
    total[...] = jnp.zeros_like(total)

    def spread(group, carry):
        terms = []
        for k in range(STEP):
            row = group * STEP + k
            rows = pl.ds(pl.multiple_of(row * BS, BS), BS)
            terms.append(jnp.dot(turned_ref[row], back_ref[rows, :], preferred_element_type=F32))
        for k in range(STEP):
            row = group * STEP + k
            total[row] += terms[k][:BS]
            total[other_ref[row]] += terms[k][BS:]
        return carry

    lax.fori_loop(0, NB // STEP, spread, 0)

    def scale(row, carry):
        rows = pl.ds(pl.multiple_of(row * BS, BS), BS)
        delta[rows, :] = (total[row] * slope_ref[rows, :]).astype(BF16)
        return carry

    lax.fori_loop(0, NB, scale, 0, unroll=4)
    out_ref[:, 0:BS] = jnp.dot(summed_ref[...], delta[...], preferred_element_type=F32).astype(BF16)


def last_part(other, back, turned, slope, summed, second):
    return call(
        last_kernel,
        jax.ShapeDtypeStruct((X * BS, (X + 1) * BS), BF16),
        [SMEM] + [VMEM] * 5,
        VMEM,
        [pltpu.VMEM((NB, BS, BS), F32), pltpu.VMEM((ROWS, BS), BF16)],
        (2 * NB * 2 * BS**3 + 2 * ROWS * 512 * BS, 8 * 1024 * 1024, 0),
        "last_part",
    )(other, back, turned, slope, summed, second)


def sum_kernel(got_ref, held_ref, out_ref, passed_ref):
    del held_ref, passed_ref
    rows = got_ref.shape[1]
    second = got_ref[0, :, BS:].astype(F32)
    for k in range(1, X * G):
        second += got_ref[k, :, BS:].astype(F32)
    for x in range(X):
        first = got_ref[x * G, :, :BS].astype(F32)
        for k in range(1, G):
            first += got_ref[x * G + k, :, :BS].astype(F32)
        for z in range(Z):
            out_ref[z, :rows, x * BS : (x + 1) * BS] = first.astype(BF16)
    for z in range(Z):
        out_ref[z, rows:, :] = second.astype(BF16)


def sum_parts(got, held):
    return pl.pallas_call(
        sum_kernel,
        out_shape=(
            jax.ShapeDtypeStruct((Z, 2 * got.shape[1], X * BS), BF16),
            jax.ShapeDtypeStruct(held.shape, held.dtype),
        ),
        in_specs=[VMEM, ANY],
        out_specs=(VMEM, ANY),
        input_output_aliases={1: 1},
        compiler_params=pltpu.CompilerParams(vmem_limit_bytes=LIMIT),
        cost_estimate=pl.CostEstimate(flops=0, bytes_accessed=1024 * 1024, transcendentals=0),
        name="sum_parts",
    )(got, held)


def assemble_kernel(x_ref, *refs):
    quarters, (out_ref, sem) = refs[:X], refs[X:]
    for k in range(X):
        rows = pl.ds(pl.multiple_of(lax.rem(x_ref[0] + X - k, X) * QUARTER, QUARTER), QUARTER)
        pltpu.make_async_copy(quarters[k], out_ref.at[rows], sem).start()
    pltpu.make_async_copy(out_ref, out_ref, sem).wait()


def assemble(my_x, quarters):
    return call(
        assemble_kernel,
        jax.ShapeDtypeStruct((ROWS, BS), BF16),
        [SMEM] + [VMEM] * X,
        ANY,
        [pltpu.SemaphoreType.DMA],
        (0, 2 * 1024 * 1024, 0),
        "assemble",
    )(my_x, *quarters)


def shift(value, step):
    return lax.ppermute(value, "z", [(i, (i + step) % Z) for i in range(Z)])


def turn(value, step):
    return lax.ppermute(value, "mp", [(i, (i + step) % X) for i in range(X)])


def gather_features(value):
    left, right = turn(value, 1), turn(value, -1)
    half = value.shape[0] // 2
    far = [turn(left[:half], 1), turn(right[half:], -1)]
    return value, left, right, far[0], far[1]


def exchange(value, axes):
    return lax.all_to_all(value, axes, split_axis=0, concat_axis=0, tiled=True)


def plane(staged):
    per = staged.shape[0] // G
    got = exchange(staged.reshape(G, per * BS, BS), ("y", "core"))
    return got.reshape(staged.shape)


def apart(work, my_z, *args):
    def skip(*args):
        return jax.tree.map(lambda leaf: jnp.zeros(leaf.shape, leaf.dtype), shapes)

    shapes = jax.eval_shape(work, *args)
    return lax.cond(my_z < Z, work, skip, *args)


def body(
    input_history,
    hidden_history,
    batch_blocks,
    tile_columns,
    tile_values,
    send_blocks,
    send_counts,
    weight_first,
    weight_second,
    cotangent,
):
    my_z = lax.axis_index("z").astype(jnp.int32)
    my_x = lax.axis_index("mp").astype(jnp.int32)
    blocks = send_blocks[0].T
    other = tile_columns[:, 1]
    table_input = pack(blocks, send_counts, input_history)

    def hop(pair):
        return shift(pair[0], 1), shift(pair[1], -1)

    def far_hop(pair):
        return shift(pair[0][:MIDDLE], 1), shift(pair[1][MIDDLE:], -1)

    def send(*sources, after=()):
        return plane(stage(my_z.reshape(1), [s if isinstance(s, tuple) else (s,) for s in sources], after))

    def beside(*sources, after=()):
        return apart(lambda sources, after: send(*sources, after=after), my_z, sources, after)

    def step_zero(table, blocks, counts, history, first, second):
        weight = jnp.concatenate([first, second])
        return hop((table, table)), beside(table), pack(blocks, counts, history), weight

    def step_one(pair, other):
        return hop(pair), hop((other, other)), beside(*pair, other)

    def step_two(pair, other):
        return hop(pair), hop(other), beside(*pair, other[0])

    def step_three(pair, other):
        return far_hop(pair), hop(other), beside(*pair, other[0])

    def step_four(far, other, after):
        return far_hop(other), beside(far, after=after)

    one, piece0, table_hidden, weight = apart(
        step_zero, my_z, table_input, blocks, send_counts, hidden_history, weight_first, weight_second
    )
    weights = lax.all_gather(weight, "mp", axis=0, tiled=False)
    cot = lax.all_gather(cotangent, "mp", axis=0, tiled=False)
    cot_rows = lax.dynamic_slice(cot, (0, my_x * QUARTER, 0), (X, QUARTER, BS))
    order = jnp.stack([my_x, (my_x - 1) % X, (my_x + 1) % X, (my_x + 2) % X])
    columns = lax.dynamic_slice(weights, (0, 0, my_x * BS), (X, BS, BS))[order].reshape(X * BS, BS)
    weight_all = weights[:, BS:].reshape(X * BS, X * BS)

    two, one_hidden, piece1 = apart(step_one, my_z, one, table_hidden)
    three, two_hidden, piece2 = apart(step_two, my_z, two, one_hidden)
    far, three_hidden, piece3 = apart(step_three, my_z, three, two_hidden)
    far_hidden, piece4 = apart(step_four, my_z, far, three_hidden, (weights, cot))

    sides_input = ((0, 0, 1), (1, 1, 3), (2, 1, 3), (3, 1, 3), (4, 0, 1), (3, 0, 3), (2, 0, 3), (1, 0, 3))
    sides_hidden = ((0, 2, 3), (3, 4, 5), (3, 3, 5), (3, 2, 5), (3, 0, 5), (3, 1, 5), (2, 2, 3), (1, 2, 3))
    use = tile_columns[:, 2:] - NB
    owner, slot = use // CAP, use % CAP
    group = (owner // (Z * C)) * C + owner % C
    code = (((owner // C) % Z - my_z) % Z * 256 + group * 8 + slot).reshape(-1)

    batch = batch_blocks.reshape(-1)
    halo_input = (piece0, piece1, piece2, piece3, piece4)
    summed_first = aggregate(sides_input, HEAD, table_input, halo_input, tile_values, code, other, batch)
    piece5 = send(far_hidden, *three_hidden, two_hidden[1], one_hidden[1], after=(summed_first,))
    halo_hidden = (piece1, piece2, piece3, piece5)
    all_first = gather_features(summed_first)
    hidden_first, slope_first = first_layer(all_first, columns)
    turned_tiles = turn_local(tile_values, summed_first)
    turned_first = prepare(my_x.reshape(1), all_first)
    summed_second = aggregate(sides_hidden, 0, hidden_first, halo_hidden, tile_values, code, other, batch)
    rows_second = exchange(summed_second.reshape(X, QUARTER, BS), "mp")
    out_rows, part_second, back_rows = second_layer(
        my_x.reshape(1), rows_second, weight_all, cot_rows, turned_first
    )
    back_second = exchange(back_rows, "mp").reshape(ROWS, BS)
    got = last_part(other, back_second, turned_tiles, slope_first, turned_first, part_second)

    dealt = X * G
    got = exchange(got.reshape(dealt, -1, (X + 1) * BS), ("mp", "y", "core"))
    parts, out_rows = sum_parts(got, out_rows)
    quarters = [out_rows[0]] + [turn(out_rows[k], k) for k in range(1, X)]
    layer_out = assemble(my_x.reshape(1), quarters)
    both = exchange(parts, "z").astype(F32).sum(0).astype(BF16)
    both = exchange(jnp.broadcast_to(both[None], (G,) + both.shape), ("y", "core"))
    both = both.reshape(G, 2, -1, X * BS).astype(F32)
    grad_first = both[:, 0].reshape(BS, X * BS)
    grad_second = both[:, 1].reshape(BS, X * BS)
    return (layer_out, grad_first, grad_second)


def solution(mesh):
    inner = Mesh(mesh.devices.reshape(Y, Z, C, X), ("y", "z", "core", "mp"))
    nodes = ("y", "z", "core")
    placed = (
        P(nodes, "mp"),
        P(nodes, "mp"),
        P(nodes, None),
        P(nodes, None),
        P(nodes, None, None, None),
        P(nodes, None, None),
        P(nodes, None),
        P("mp", None),
        P("mp", None),
        P(nodes, "mp"),
    )
    return jax.shard_map(
        body,
        mesh=inner,
        in_specs=placed,
        out_specs=(P(nodes, "mp"), P("mp", None), P("mp", None)),
        check_vma=False,
    )
```

```python
import functools

import jax
import jax.numpy as jnp
from jax import lax
from jax.experimental import pallas as pl
from jax.experimental.pallas import tpu as pltpu
from jax.sharding import Mesh
from jax.sharding import PartitionSpec as P

Y, Z, C, X = 4, 8, 2, 4
G = Y * C
BS = 128
NB = 24
TPR = 5
CAP = 3
HB = 32
ROWS = NB * BS
QUARTER = ROWS // X
STEP = 4
F32 = jnp.float32
BF16 = jnp.bfloat16
ANY = pl.BlockSpec(memory_space=pltpu.HBM)
VMEM = pl.BlockSpec(memory_space=pltpu.VMEM)
SMEM = pl.BlockSpec(memory_space=pltpu.SMEM)
LIMIT = 48 * 1024 * 1024


def call(kernel, out_shape, in_specs, out_specs, scratch, cost, name):
    return pl.pallas_call(
        kernel,
        out_shape=out_shape,
        in_specs=in_specs,
        out_specs=out_specs,
        scratch_shapes=scratch,
        compiler_params=pltpu.CompilerParams(vmem_limit_bytes=LIMIT),
        cost_estimate=pl.CostEstimate(flops=cost[0], bytes_accessed=cost[1], transcendentals=cost[2]),
        name=name,
    )


HEAD = 16
HALF = HB // 2
MIDDLE = HEAD + HALF * BS


def pack_kernel(blocks_ref, counts_ref, history_ref, out_ref, wanted, rows_in, sem):
    parts = sem.shape[0]
    size = HB * BS // parts
    copies = [
        pltpu.make_async_copy(history_ref.at[pl.ds(k * size, size)], rows_in.at[pl.ds(k * size, size)], sem.at[k])
        for k in range(parts)
    ]
    for copy in copies:
        copy.start()
    wanted[...] = jnp.zeros_like(wanted)
    blocks = blocks_ref[...]
    slot = lax.broadcasted_iota(jnp.int32, blocks.shape, 0)
    wanted[0:CAP, 0 : blocks.shape[1]] = jnp.where(slot < counts_ref[...], blocks, HB)
    out_ref[0:HEAD, :] = wanted[...].astype(F32).astype(BF16)
    for k in range(parts):
        copies[k].wait()

        def one(block, carry, k=k):
            rows = pl.multiple_of(k * size + block * BS, BS)
            out_ref[pl.ds(pl.multiple_of(HEAD + rows, HEAD), BS), :] = rows_in[pl.ds(rows, BS), :].astype(BF16)
            return carry

        lax.fori_loop(0, size // BS, one, 0, unroll=2)


def pack(blocks, counts, history):
    return call(
        pack_kernel,
        jax.ShapeDtypeStruct((HEAD + HB * BS, BS), BF16),
        [VMEM, VMEM, ANY],
        VMEM,
        [
            pltpu.VMEM((HEAD, BS), jnp.int32),
            pltpu.VMEM(history.shape, F32),
            pltpu.SemaphoreType.DMA((4,)),
        ],
        (0, 3 * 1024 * 1024, 0),
        "pack",
    )(blocks, counts, history)


def stage_kernel(sizes, z_ref, *refs):
    count = len(sizes)
    total = sum(sizes)
    flat, (out_ref, ints, asked, sem) = refs[:total], refs[-4:]
    sources = [flat[sum(sizes[:s]) : sum(sizes[: s + 1])] for s in range(count)]
    copies = [pltpu.make_async_copy(ints.at[s], asked.at[s], sem.at[s]) for s in range(count)]
    for s in range(count):
        ints[s] = sources[s][0][0:HEAD, :].astype(F32).astype(jnp.int32)
        copies[s].start()
    for copy in copies:
        copy.wait()
    mine = z_ref[0]
    zeros = jnp.zeros((BS, BS), BF16)

    def block_of(source, block):
        if len(source) == 1:
            start = pl.multiple_of(HEAD + jnp.minimum(block, HB - 1) * BS, HEAD)
            return jnp.where(block < HB, source[0][pl.ds(start, BS), :], zeros)
        first = pl.multiple_of(HEAD + jnp.minimum(block, HALF - 1) * BS, HEAD)
        second = pl.multiple_of(jnp.clip(block - HALF, 0, HALF - 1) * BS, BS)
        late = jnp.where(block < HB, source[1][pl.ds(second, BS), :], zeros)
        return jnp.where(block < HALF, source[0][pl.ds(first, BS), :], late)

    def one(reader, carry):
        column = (reader // C) * (Z * C) + mine * C + lax.rem(reader, C)
        for s, source in enumerate(sources):
            found = [block_of(source, asked[s, slot, column]) for slot in range(CAP)]
            for slot in range(CAP):
                out_ref[(reader * count + s) * CAP + slot] = found[slot]
        return carry

    lax.fori_loop(0, G, one, 0)


def stage(my_z, sources, after=()):
    count = len(sources)
    sizes = tuple(len(source) for source in sources)
    entries = G * CAP * count
    return call(
        functools.partial(stage_kernel, sizes),
        jax.ShapeDtypeStruct((entries, BS, BS), BF16),
        [SMEM] + [VMEM] * sum(sizes) + [ANY] * len(after),
        VMEM,
        [
            pltpu.VMEM((count, HEAD, BS), jnp.int32),
            pltpu.SMEM((count, HEAD, BS), jnp.int32),
            pltpu.SemaphoreType.DMA((count,)),
        ],
        (0, 2 * entries * BS * BS * 2, 0),
        "stage",
    )(my_z, *[part for source in sources for part in source], *after)


def aggregate_kernel(sides, count, skip, code_ref, other_ref, blocks_ref, table, tiles, *refs):
    halos, (out_ref, halo, sem) = refs[:count], refs[count:]

    def local(row):
        pair = (row, other_ref[row])
        return [blocks_ref[block] for block in pair] if skip else pair

    def start(row, carry):
        for slot in range(TPR - 2):
            code = code_ref[row * (TPR - 2) + slot]
            distance, group, number = code >> 8, (code >> 3) & 31, code & 7
            for side, (piece, source, sources) in enumerate(sides):

                @pl.when(distance == side)
                def _(piece=piece, source=source, sources=sources, group=group, number=number, slot=slot):
                    place = (group * sources + source) * CAP + number
                    pltpu.make_async_copy(halos[piece].at[place], halo.at[row, slot], sem.at[row >> 2]).start()

        return carry

    lax.fori_loop(0, NB, start, 0)

    def compute(group, carry):
        rows = pl.ds(group * STEP, STEP)
        pltpu.make_async_copy(halo.at[rows], halo.at[rows], sem.at[group]).wait()
        for k in range(STEP):
            row = group * STEP + k
            left = jnp.concatenate([tiles[row, t] for t in range(TPR)], axis=1)
            right = jnp.concatenate(
                [table[pl.ds(pl.multiple_of(skip + block * BS, HEAD), BS), :] for block in local(row)]
                + [halo[row, t] for t in range(TPR - 2)],
                axis=0,
            )
            summed = jnp.dot(left, right, preferred_element_type=F32)
            out_ref[pl.ds(pl.multiple_of(row * BS, BS), BS), :] = summed.astype(BF16)
        return carry

    lax.fori_loop(0, NB // STEP, compute, 0)


def aggregate(sides, skip, table, halos, tiles, code, other, blocks):
    return call(
        functools.partial(aggregate_kernel, sides, len(halos), skip),
        jax.ShapeDtypeStruct((ROWS, BS), BF16),
        [SMEM] * 3 + [VMEM] * 2 + [ANY] * len(halos),
        VMEM,
        [pltpu.VMEM((NB, TPR - 2, BS, BS), BF16), pltpu.SemaphoreType.DMA((NB // STEP,))],
        (2 * NB * TPR * BS**3, 2 * NB * TPR * BS * BS * 2, 0),
        "aggregate",
    )(code, other, blocks, table, tiles, *halos)


def sigmoid(value):
    return 1.0 / (1.0 + jnp.exp(-value))


def first_kernel(s0, s1, s2, far0, far1, weight_ref, hidden_ref, slope_ref):
    weight = weight_ref[...]
    step = 256
    half = ROWS // 2 // step

    def one(far, begin, row, carry):
        rows = pl.ds(pl.multiple_of((row + begin) * step, step), step)
        far_rows = pl.ds(pl.multiple_of(row * step, step), step)
        left = jnp.concatenate([s0[rows, :], s1[rows, :], s2[rows, :], far[far_rows, :]], axis=1)
        pre = jnp.dot(left, weight, preferred_element_type=F32)
        sig = sigmoid(pre)
        hidden_ref[rows, :] = (pre * sig).astype(BF16)
        slope_ref[rows, :] = sig * (1.0 + pre * (1.0 - sig))
        return carry

    lax.fori_loop(0, half, functools.partial(one, far0, 0), 0)
    lax.fori_loop(0, half, functools.partial(one, far1, half), 0)


def first_layer(summed, weight):
    return call(
        first_kernel,
        (jax.ShapeDtypeStruct((ROWS, BS), BF16), jax.ShapeDtypeStruct((ROWS, BS), F32)),
        [VMEM] * 6,
        (VMEM, VMEM),
        [],
        (2 * ROWS * 512 * BS, 6 * 1024 * 1024, ROWS * BS),
        "first_layer",
    )(*summed, weight)


def second_kernel(x_ref, summed_ref, weight_ref, cot_ref, after_ref, out_ref, grad_ref, back_ref, delta_ref):
    del after_ref
    step = 128

    def one(row, carry):
        rows = pl.ds(pl.multiple_of(row * step, step), step)
        left = jnp.concatenate([summed_ref[k, rows, :] for k in range(X)], axis=1)
        cot = jnp.concatenate([cot_ref[k, rows, :] for k in range(X)], axis=1)
        pre = jnp.dot(left, weight_ref[...], preferred_element_type=F32)
        sig = sigmoid(pre)
        out = (pre * sig).astype(BF16)
        delta = (cot.astype(F32) * (sig * (1.0 + pre * (1.0 - sig)))).astype(BF16)
        back = lax.dot_general(
            delta, weight_ref[...], (((1,), (1,)), ((), ())), preferred_element_type=F32
        ).astype(BF16)
        delta_ref[rows, :] = delta
        for k in range(X):
            out_ref[lax.rem(k + X - x_ref[0], X), rows, :] = out[:, k * BS : (k + 1) * BS]
            back_ref[k, rows, :] = back[:, k * BS : (k + 1) * BS]
        return carry

    lax.fori_loop(0, QUARTER // step, one, 0)
    for k in range(X):
        grad_ref[k * BS : (k + 1) * BS, :] = lax.dot_general(
            summed_ref[k], delta_ref[...], (((0,), (0,)), ((), ())), preferred_element_type=F32
        ).astype(BF16)


def second_layer(my_x, summed, weight, cot, after):
    piece = jax.ShapeDtypeStruct((X, QUARTER, BS), BF16)
    return call(
        second_kernel,
        (piece, jax.ShapeDtypeStruct((X * BS, X * BS), BF16), piece),
        [SMEM] + [VMEM] * 3 + [ANY],
        (VMEM,) * 3,
        [pltpu.VMEM((QUARTER, X * BS), BF16)],
        (6 * QUARTER * 512 * 512, 5 * 1024 * 1024, QUARTER * 512),
        "second_layer",
    )(my_x, summed, weight, cot, after)


def turn_kernel(tiles_ref, after_ref, turned_ref, tiles, sem):
    del after_ref

    def start(row, carry):
        pltpu.make_async_copy(tiles_ref.at[row, pl.ds(0, 2)], tiles.at[row], sem).start()
        return carry

    lax.fori_loop(0, NB, start, 0)
    pltpu.make_async_copy(tiles, tiles, sem).wait()

    def turn_tiles(row, carry):
        for t in range(2):
            turned_ref[row, pl.ds(t * BS, BS), :] = tiles[row, t].T
        return carry

    lax.fori_loop(0, NB, turn_tiles, 0, unroll=2)


def turn_local(tiles, after):
    return call(
        turn_kernel,
        jax.ShapeDtypeStruct((NB, 2 * BS, BS), BF16),
        [ANY, ANY],
        VMEM,
        [pltpu.VMEM((NB, 2, BS, BS), BF16), pltpu.SemaphoreType.DMA],
        (0, 4 * 1024 * 1024, 0),
        "turn_local",
    )(tiles, after)


def prepare_kernel(x_ref, s0, s1, s2, far0, far1, summed_ref):
    x = x_ref[0]
    half = ROWS // 2
    for source, step, begin in ((s0, 0, 0), (s1, X - 1, 0), (s2, 1, 0), (far0, 2, 0), (far1, 2, half)):
        place = pl.ds(pl.multiple_of(lax.rem(x + step, X) * BS, BS), BS)

        def one(block, carry, source=source, begin=begin, place=place):
            rows = pl.ds(pl.multiple_of(block * BS, BS), BS)
            columns = pl.ds(pl.multiple_of(begin + block * BS, BS), BS)
            summed_ref[place, columns] = source[rows, :].T
            return carry

        lax.fori_loop(0, source.shape[0] // BS, one, 0, unroll=4)


def prepare(my_x, summed):
    return call(
        prepare_kernel,
        jax.ShapeDtypeStruct((X * BS, ROWS), BF16),
        [SMEM] + [VMEM] * 5,
        VMEM,
        [],
        (0, 7 * 1024 * 1024, 0),
        "prepare",
    )(my_x, *summed)


def last_kernel(other_ref, back_ref, turned_ref, slope_ref, summed_ref, second_ref, out_ref, total, delta):
    out_ref[:, BS:] = second_ref[...]
    total[...] = jnp.zeros_like(total)

    def spread(group, carry):
        terms = []
        for k in range(STEP):
            row = group * STEP + k
            rows = pl.ds(pl.multiple_of(row * BS, BS), BS)
            terms.append(jnp.dot(turned_ref[row], back_ref[rows, :], preferred_element_type=F32))
        for k in range(STEP):
            row = group * STEP + k
            total[row] += terms[k][:BS]
            total[other_ref[row]] += terms[k][BS:]
        return carry

    lax.fori_loop(0, NB // STEP, spread, 0)

    def scale(row, carry):
        rows = pl.ds(pl.multiple_of(row * BS, BS), BS)
        delta[rows, :] = (total[row] * slope_ref[rows, :]).astype(BF16)
        return carry

    lax.fori_loop(0, NB, scale, 0, unroll=4)
    out_ref[:, 0:BS] = jnp.dot(summed_ref[...], delta[...], preferred_element_type=F32).astype(BF16)


def last_part(other, back, turned, slope, summed, second):
    return call(
        last_kernel,
        jax.ShapeDtypeStruct((X * BS, (X + 1) * BS), BF16),
        [SMEM] + [VMEM] * 5,
        VMEM,
        [pltpu.VMEM((NB, BS, BS), F32), pltpu.VMEM((ROWS, BS), BF16)],
        (2 * NB * 2 * BS**3 + 2 * ROWS * 512 * BS, 8 * 1024 * 1024, 0),
        "last_part",
    )(other, back, turned, slope, summed, second)


def sum_kernel(got_ref, held_ref, out_ref, passed_ref):
    del held_ref, passed_ref
    rows = got_ref.shape[1]
    second = got_ref[0, :, BS:].astype(F32)
    for k in range(1, X * G):
        second += got_ref[k, :, BS:].astype(F32)
    for x in range(X):
        first = got_ref[x * G, :, :BS].astype(F32)
        for k in range(1, G):
            first += got_ref[x * G + k, :, :BS].astype(F32)
        for z in range(Z):
            out_ref[z, :rows, x * BS : (x + 1) * BS] = first.astype(BF16)
    for z in range(Z):
        out_ref[z, rows:, :] = second.astype(BF16)


def sum_parts(got, held):
    return pl.pallas_call(
        sum_kernel,
        out_shape=(
            jax.ShapeDtypeStruct((Z, 2 * got.shape[1], X * BS), BF16),
            jax.ShapeDtypeStruct(held.shape, held.dtype),
        ),
        in_specs=[VMEM, ANY],
        out_specs=(VMEM, ANY),
        input_output_aliases={1: 1},
        compiler_params=pltpu.CompilerParams(vmem_limit_bytes=LIMIT),
        cost_estimate=pl.CostEstimate(flops=0, bytes_accessed=1024 * 1024, transcendentals=0),
        name="sum_parts",
    )(got, held)


def planes_kernel(parts_ref, after_ref, out_ref):
    del after_ref
    total = parts_ref[0].astype(F32)
    for z in range(1, Z):
        total += parts_ref[z].astype(F32)
    for reader in range(G):
        out_ref[reader] = total.astype(BF16)


def sum_planes(parts, after):
    return call(
        planes_kernel,
        jax.ShapeDtypeStruct((G,) + parts.shape[1:], BF16),
        [VMEM, ANY],
        VMEM,
        [],
        (0, 1024 * 1024, 0),
        "sum_planes",
    )(parts, after)


def assemble_kernel(x_ref, *refs):
    quarters, (out_ref, sem) = refs[:X], refs[X:]
    for k in range(X):
        rows = pl.ds(pl.multiple_of(lax.rem(x_ref[0] + X - k, X) * QUARTER, QUARTER), QUARTER)
        pltpu.make_async_copy(quarters[k], out_ref.at[rows], sem).start()
    pltpu.make_async_copy(out_ref, out_ref, sem).wait()


def assemble(my_x, quarters):
    return call(
        assemble_kernel,
        jax.ShapeDtypeStruct((ROWS, BS), BF16),
        [SMEM] + [VMEM] * X,
        ANY,
        [pltpu.SemaphoreType.DMA],
        (0, 2 * 1024 * 1024, 0),
        "assemble",
    )(my_x, *quarters)


def shift(value, step):
    return lax.ppermute(value, "z", [(i, (i + step) % Z) for i in range(Z)])


def turn(value, step):
    return lax.ppermute(value, "mp", [(i, (i + step) % X) for i in range(X)])


def gather_features(value):
    left, right = turn(value, 1), turn(value, -1)
    half = value.shape[0] // 2
    far = [turn(left[:half], 1), turn(right[half:], -1)]
    return value, left, right, far[0], far[1]


def exchange(value, axes):
    return lax.all_to_all(value, axes, split_axis=0, concat_axis=0, tiled=True)


def plane(staged):
    per = staged.shape[0] // G
    got = exchange(staged.reshape(G, per * BS, BS), ("y", "core"))
    return got.reshape(staged.shape)


def apart(work, my_z, *args):
    def skip(*args):
        return jax.tree.map(lambda leaf: jnp.zeros(leaf.shape, leaf.dtype), shapes)

    shapes = jax.eval_shape(work, *args)
    return lax.cond(my_z < Z, work, skip, *args)


def body(
    input_history,
    hidden_history,
    batch_blocks,
    tile_columns,
    tile_values,
    send_blocks,
    send_counts,
    weight_first,
    weight_second,
    cotangent,
):
    my_z = lax.axis_index("z").astype(jnp.int32)
    my_x = lax.axis_index("mp").astype(jnp.int32)
    blocks = send_blocks[0].T
    other = tile_columns[:, 1]
    table_input = pack(blocks, send_counts, input_history)

    def hop(pair):
        return shift(pair[0], 1), shift(pair[1], -1)

    def far_hop(pair):
        return shift(pair[0][:MIDDLE], 1), shift(pair[1][MIDDLE:], -1)

    def send(*sources, after=()):
        return plane(stage(my_z.reshape(1), [s if isinstance(s, tuple) else (s,) for s in sources], after))

    def beside(*sources, after=()):
        return apart(lambda sources, after: send(*sources, after=after), my_z, sources, after)

    def step_zero(table, blocks, counts, history, first, second):
        weight = jnp.concatenate([first, second])
        return hop((table, table)), beside(table), pack(blocks, counts, history), weight

    def step_one(pair, other):
        return hop(pair), hop((other, other)), beside(*pair, other)

    def step_two(pair, other):
        return hop(pair), hop(other), beside(*pair, other[0])

    def step_three(pair, other):
        return far_hop(pair), hop(other), beside(*pair, other[0])

    def step_four(far, other, after):
        return far_hop(other), beside(far, after=after)

    one, piece0, table_hidden, weight = apart(
        step_zero, my_z, table_input, blocks, send_counts, hidden_history, weight_first, weight_second
    )
    weights = lax.all_gather(weight, "mp", axis=0, tiled=False)
    cot = lax.all_gather(cotangent, "mp", axis=0, tiled=False)
    cot_rows = lax.dynamic_slice(cot, (0, my_x * QUARTER, 0), (X, QUARTER, BS))
    order = jnp.stack([my_x, (my_x - 1) % X, (my_x + 1) % X, (my_x + 2) % X])
    columns = lax.dynamic_slice(weights, (0, 0, my_x * BS), (X, BS, BS))[order].reshape(X * BS, BS)
    weight_all = weights[:, BS:].reshape(X * BS, X * BS)

    two, one_hidden, piece1 = apart(step_one, my_z, one, table_hidden)
    three, two_hidden, piece2 = apart(step_two, my_z, two, one_hidden)
    far, three_hidden, piece3 = apart(step_three, my_z, three, two_hidden)
    far_hidden, piece4 = apart(step_four, my_z, far, three_hidden, (weights, cot))

    sides_input = ((0, 0, 1), (1, 1, 3), (2, 1, 3), (3, 1, 3), (4, 0, 1), (3, 0, 3), (2, 0, 3), (1, 0, 3))
    sides_hidden = ((0, 2, 3), (3, 4, 5), (3, 3, 5), (3, 2, 5), (3, 0, 5), (3, 1, 5), (2, 2, 3), (1, 2, 3))
    use = tile_columns[:, 2:] - NB
    owner, slot = use // CAP, use % CAP
    group = (owner // (Z * C)) * C + owner % C
    code = (((owner // C) % Z - my_z) % Z * 256 + group * 8 + slot).reshape(-1)

    batch = batch_blocks.reshape(-1)
    halo_input = (piece0, piece1, piece2, piece3, piece4)
    summed_first = aggregate(sides_input, HEAD, table_input, halo_input, tile_values, code, other, batch)
    piece5 = send(far_hidden, *three_hidden, two_hidden[1], one_hidden[1], after=(summed_first,))
    halo_hidden = (piece1, piece2, piece3, piece5)
    all_first = gather_features(summed_first)
    hidden_first, slope_first = first_layer(all_first, columns)
    turned_tiles = turn_local(tile_values, summed_first)
    turned_first = prepare(my_x.reshape(1), all_first)
    summed_second = aggregate(sides_hidden, 0, hidden_first, halo_hidden, tile_values, code, other, batch)
    rows_second = exchange(summed_second.reshape(X, QUARTER, BS), "mp")
    out_rows, part_second, back_rows = second_layer(
        my_x.reshape(1), rows_second, weight_all, cot_rows, turned_first
    )
    back_second = exchange(back_rows, "mp").reshape(ROWS, BS)
    got = last_part(other, back_second, turned_tiles, slope_first, turned_first, part_second)

    dealt = X * G
    got = exchange(got.reshape(dealt, -1, (X + 1) * BS), ("mp", "y", "core"))
    parts, out_rows = sum_parts(got, out_rows)
    quarters = [out_rows[0]] + [turn(out_rows[k], k) for k in range(1, X)]
    layer_out = assemble(my_x.reshape(1), quarters)
    both = exchange(sum_planes(exchange(parts, "z"), layer_out), ("y", "core"))
    both = both.reshape(G, 2, -1, X * BS).astype(F32)
    grad_first = both[:, 0].reshape(BS, X * BS)
    grad_second = both[:, 1].reshape(BS, X * BS)
    return (layer_out, grad_first, grad_second)


def solution(mesh):
    inner = Mesh(mesh.devices.reshape(Y, Z, C, X), ("y", "z", "core", "mp"))
    nodes = ("y", "z", "core")
    placed = (
        P(nodes, "mp"),
        P(nodes, "mp"),
        P(nodes, None),
        P(nodes, None),
        P(nodes, None, None, None),
        P(nodes, None, None),
        P(nodes, None),
        P("mp", None),
        P("mp", None),
        P(nodes, "mp"),
    )
    return jax.shard_map(
        body,
        mesh=inner,
        in_specs=placed,
        out_specs=(P(nodes, "mp"), P("mp", None), P("mp", None)),
        check_vma=False,
    )
```

```python
import functools

import jax
import jax.numpy as jnp
from jax import lax
from jax.experimental import pallas as pl
from jax.experimental.pallas import tpu as pltpu
from jax.sharding import Mesh
from jax.sharding import PartitionSpec as P

Y, Z, C, X = 4, 8, 2, 4
G = Y * C
BS = 128
NB = 24
TPR = 5
CAP = 3
HB = 32
ROWS = NB * BS
QUARTER = ROWS // X
STEP = 4
F32 = jnp.float32
BF16 = jnp.bfloat16
ANY = pl.BlockSpec(memory_space=pltpu.HBM)
VMEM = pl.BlockSpec(memory_space=pltpu.VMEM)
SMEM = pl.BlockSpec(memory_space=pltpu.SMEM)
LIMIT = 48 * 1024 * 1024


def call(kernel, out_shape, in_specs, out_specs, scratch, cost, name):
    return pl.pallas_call(
        kernel,
        out_shape=out_shape,
        in_specs=in_specs,
        out_specs=out_specs,
        scratch_shapes=scratch,
        compiler_params=pltpu.CompilerParams(vmem_limit_bytes=LIMIT),
        cost_estimate=pl.CostEstimate(flops=cost[0], bytes_accessed=cost[1], transcendentals=cost[2]),
        name=name,
    )


HEAD = 16
HALF = HB // 2
MIDDLE = HEAD + HALF * BS


def pack_kernel(blocks_ref, counts_ref, history_ref, out_ref, wanted, rows_in, sem):
    parts = sem.shape[0]
    size = HB * BS // parts
    copies = [
        pltpu.make_async_copy(history_ref.at[pl.ds(k * size, size)], rows_in.at[pl.ds(k * size, size)], sem.at[k])
        for k in range(parts)
    ]
    for copy in copies:
        copy.start()
    wanted[...] = jnp.zeros_like(wanted)
    blocks = blocks_ref[...]
    slot = lax.broadcasted_iota(jnp.int32, blocks.shape, 0)
    wanted[0:CAP, 0 : blocks.shape[1]] = jnp.where(slot < counts_ref[...], blocks, HB)
    out_ref[0:HEAD, :] = wanted[...].astype(F32).astype(BF16)
    for k in range(parts):
        copies[k].wait()

        def one(block, carry, k=k):
            rows = pl.multiple_of(k * size + block * BS, BS)
            out_ref[pl.ds(pl.multiple_of(HEAD + rows, HEAD), BS), :] = rows_in[pl.ds(rows, BS), :].astype(BF16)
            return carry

        lax.fori_loop(0, size // BS, one, 0, unroll=2)


def pack(blocks, counts, history):
    return call(
        pack_kernel,
        jax.ShapeDtypeStruct((HEAD + HB * BS, BS), BF16),
        [VMEM, VMEM, ANY],
        VMEM,
        [
            pltpu.VMEM((HEAD, BS), jnp.int32),
            pltpu.VMEM(history.shape, F32),
            pltpu.SemaphoreType.DMA((4,)),
        ],
        (0, 3 * 1024 * 1024, 0),
        "pack",
    )(blocks, counts, history)


def stage_kernel(sizes, z_ref, *refs):
    count = len(sizes)
    total = sum(sizes)
    flat, (out_ref, ints, asked, sem) = refs[:total], refs[-4:]
    sources = [flat[sum(sizes[:s]) : sum(sizes[: s + 1])] for s in range(count)]
    copies = [pltpu.make_async_copy(ints.at[s], asked.at[s], sem.at[s]) for s in range(count)]
    for s in range(count):
        ints[s] = sources[s][0][0:HEAD, :].astype(F32).astype(jnp.int32)
        copies[s].start()
    for copy in copies:
        copy.wait()
    mine = z_ref[0]
    zeros = jnp.zeros((BS, BS), BF16)

    def block_of(source, block):
        if len(source) == 1:
            start = pl.multiple_of(HEAD + jnp.minimum(block, HB - 1) * BS, HEAD)
            return jnp.where(block < HB, source[0][pl.ds(start, BS), :], zeros)
        first = pl.multiple_of(HEAD + jnp.minimum(block, HALF - 1) * BS, HEAD)
        second = pl.multiple_of(jnp.clip(block - HALF, 0, HALF - 1) * BS, BS)
        late = jnp.where(block < HB, source[1][pl.ds(second, BS), :], zeros)
        return jnp.where(block < HALF, source[0][pl.ds(first, BS), :], late)

    def one(reader, carry):
        column = (reader // C) * (Z * C) + mine * C + lax.rem(reader, C)
        for s, source in enumerate(sources):
            found = [block_of(source, asked[s, slot, column]) for slot in range(CAP)]
            for slot in range(CAP):
                out_ref[(reader * count + s) * CAP + slot] = found[slot]
        return carry

    lax.fori_loop(0, G, one, 0)


def stage(my_z, sources, after=()):
    count = len(sources)
    sizes = tuple(len(source) for source in sources)
    entries = G * CAP * count
    return call(
        functools.partial(stage_kernel, sizes),
        jax.ShapeDtypeStruct((entries, BS, BS), BF16),
        [SMEM] + [VMEM] * sum(sizes) + [ANY] * len(after),
        VMEM,
        [
            pltpu.VMEM((count, HEAD, BS), jnp.int32),
            pltpu.SMEM((count, HEAD, BS), jnp.int32),
            pltpu.SemaphoreType.DMA((count,)),
        ],
        (0, 2 * entries * BS * BS * 2, 0),
        "stage",
    )(my_z, *[part for source in sources for part in source], *after)


def aggregate_kernel(sides, count, skip, code_ref, other_ref, blocks_ref, table, tiles, *refs):
    halos, (out_ref, halo, sem) = refs[:count], refs[count:]

    def local(row):
        pair = (row, other_ref[row])
        return [blocks_ref[block] for block in pair] if skip else pair

    def start(row, carry):
        for slot in range(TPR - 2):
            code = code_ref[row * (TPR - 2) + slot]
            distance, group, number = code >> 8, (code >> 3) & 31, code & 7
            for side, (piece, source, sources) in enumerate(sides):

                @pl.when(distance == side)
                def _(piece=piece, source=source, sources=sources, group=group, number=number, slot=slot):
                    place = (group * sources + source) * CAP + number
                    pltpu.make_async_copy(halos[piece].at[place], halo.at[row, slot], sem.at[row >> 2]).start()

        return carry

    lax.fori_loop(0, NB, start, 0)

    def compute(group, carry):
        rows = pl.ds(group * STEP, STEP)
        pltpu.make_async_copy(halo.at[rows], halo.at[rows], sem.at[group]).wait()
        for k in range(STEP):
            row = group * STEP + k
            left = jnp.concatenate([tiles[row, t] for t in range(TPR)], axis=1)
            right = jnp.concatenate(
                [table[pl.ds(pl.multiple_of(skip + block * BS, HEAD), BS), :] for block in local(row)]
                + [halo[row, t] for t in range(TPR - 2)],
                axis=0,
            )
            summed = jnp.dot(left, right, preferred_element_type=F32)
            out_ref[pl.ds(pl.multiple_of(row * BS, BS), BS), :] = summed.astype(BF16)
        return carry

    lax.fori_loop(0, NB // STEP, compute, 0)


def aggregate(sides, skip, table, halos, tiles, code, other, blocks):
    return call(
        functools.partial(aggregate_kernel, sides, len(halos), skip),
        jax.ShapeDtypeStruct((ROWS, BS), BF16),
        [SMEM] * 3 + [VMEM] * 2 + [ANY] * len(halos),
        VMEM,
        [pltpu.VMEM((NB, TPR - 2, BS, BS), BF16), pltpu.SemaphoreType.DMA((NB // STEP,))],
        (2 * NB * TPR * BS**3, 2 * NB * TPR * BS * BS * 2, 0),
        "aggregate",
    )(code, other, blocks, table, tiles, *halos)


def sigmoid(value):
    return 1.0 / (1.0 + jnp.exp(-value))


def first_kernel(s0, s1, s2, far0, far1, weight_ref, hidden_ref, slope_ref):
    weight = weight_ref[...]
    step = 256
    half = ROWS // 2 // step

    def one(far, begin, row, carry):
        rows = pl.ds(pl.multiple_of((row + begin) * step, step), step)
        far_rows = pl.ds(pl.multiple_of(row * step, step), step)
        left = jnp.concatenate([s0[rows, :], s1[rows, :], s2[rows, :], far[far_rows, :]], axis=1)
        pre = jnp.dot(left, weight, preferred_element_type=F32)
        sig = sigmoid(pre)
        hidden_ref[rows, :] = (pre * sig).astype(BF16)
        slope_ref[rows, :] = sig * (1.0 + pre * (1.0 - sig))
        return carry

    lax.fori_loop(0, half, functools.partial(one, far0, 0), 0)
    lax.fori_loop(0, half, functools.partial(one, far1, half), 0)


def first_layer(summed, weight):
    return call(
        first_kernel,
        (jax.ShapeDtypeStruct((ROWS, BS), BF16), jax.ShapeDtypeStruct((ROWS, BS), F32)),
        [VMEM] * 6,
        (VMEM, VMEM),
        [],
        (2 * ROWS * 512 * BS, 6 * 1024 * 1024, ROWS * BS),
        "first_layer",
    )(*summed, weight)


def second_kernel(x_ref, summed_ref, weight_ref, cot_ref, after_ref, out_ref, grad_ref, back_ref, delta_ref):
    del after_ref
    step = 128

    def one(row, carry):
        rows = pl.ds(pl.multiple_of(row * step, step), step)
        left = jnp.concatenate([summed_ref[k, rows, :] for k in range(X)], axis=1)
        cot = jnp.concatenate([cot_ref[k, rows, :] for k in range(X)], axis=1)
        pre = jnp.dot(left, weight_ref[...], preferred_element_type=F32)
        sig = sigmoid(pre)
        out = (pre * sig).astype(BF16)
        delta = (cot.astype(F32) * (sig * (1.0 + pre * (1.0 - sig)))).astype(BF16)
        back = lax.dot_general(
            delta, weight_ref[...], (((1,), (1,)), ((), ())), preferred_element_type=F32
        ).astype(BF16)
        delta_ref[rows, :] = delta
        for k in range(X):
            out_ref[lax.rem(k + X - x_ref[0], X), rows, :] = out[:, k * BS : (k + 1) * BS]
            back_ref[k, rows, :] = back[:, k * BS : (k + 1) * BS]
        return carry

    lax.fori_loop(0, QUARTER // step, one, 0)
    for k in range(X):
        grad_ref[k * BS : (k + 1) * BS, :] = lax.dot_general(
            summed_ref[k], delta_ref[...], (((0,), (0,)), ((), ())), preferred_element_type=F32
        ).astype(BF16)


def second_layer(my_x, summed, weight, cot, after):
    piece = jax.ShapeDtypeStruct((X, QUARTER, BS), BF16)
    return call(
        second_kernel,
        (piece, jax.ShapeDtypeStruct((X * BS, X * BS), BF16), piece),
        [SMEM] + [VMEM] * 3 + [ANY],
        (VMEM,) * 3,
        [pltpu.VMEM((QUARTER, X * BS), BF16)],
        (6 * QUARTER * 512 * 512, 5 * 1024 * 1024, QUARTER * 512),
        "second_layer",
    )(my_x, summed, weight, cot, after)


def turn_kernel(tiles_ref, after_ref, turned_ref, tiles, sem):
    del after_ref

    def start(row, carry):
        pltpu.make_async_copy(tiles_ref.at[row, pl.ds(0, 2)], tiles.at[row], sem).start()
        return carry

    lax.fori_loop(0, NB, start, 0)
    pltpu.make_async_copy(tiles, tiles, sem).wait()

    def turn_tiles(row, carry):
        for t in range(2):
            turned_ref[row, pl.ds(t * BS, BS), :] = tiles[row, t].T
        return carry

    lax.fori_loop(0, NB, turn_tiles, 0, unroll=2)


def turn_local(tiles, after):
    return call(
        turn_kernel,
        jax.ShapeDtypeStruct((NB, 2 * BS, BS), BF16),
        [ANY, ANY],
        VMEM,
        [pltpu.VMEM((NB, 2, BS, BS), BF16), pltpu.SemaphoreType.DMA],
        (0, 4 * 1024 * 1024, 0),
        "turn_local",
    )(tiles, after)


def prepare_kernel(x_ref, s0, s1, s2, far0, far1, summed_ref):
    x = x_ref[0]
    half = ROWS // 2
    for source, step, begin in ((s0, 0, 0), (s1, X - 1, 0), (s2, 1, 0), (far0, 2, 0), (far1, 2, half)):
        place = pl.ds(pl.multiple_of(lax.rem(x + step, X) * BS, BS), BS)

        def one(block, carry, source=source, begin=begin, place=place):
            rows = pl.ds(pl.multiple_of(block * BS, BS), BS)
            columns = pl.ds(pl.multiple_of(begin + block * BS, BS), BS)
            summed_ref[place, columns] = source[rows, :].T
            return carry

        lax.fori_loop(0, source.shape[0] // BS, one, 0, unroll=4)


def prepare(my_x, summed):
    return call(
        prepare_kernel,
        jax.ShapeDtypeStruct((X * BS, ROWS), BF16),
        [SMEM] + [VMEM] * 5,
        VMEM,
        [],
        (0, 7 * 1024 * 1024, 0),
        "prepare",
    )(my_x, *summed)


def last_kernel(other_ref, back_ref, turned_ref, slope_ref, summed_ref, second_ref, out_ref, total, delta):
    out_ref[:, BS:] = second_ref[...]
    total[...] = jnp.zeros_like(total)

    def spread(group, carry):
        terms = []
        for k in range(STEP):
            row = group * STEP + k
            rows = pl.ds(pl.multiple_of(row * BS, BS), BS)
            terms.append(jnp.dot(turned_ref[row], back_ref[rows, :], preferred_element_type=F32))
        for k in range(STEP):
            row = group * STEP + k
            total[row] += terms[k][:BS]
            total[other_ref[row]] += terms[k][BS:]
        return carry

    lax.fori_loop(0, NB // STEP, spread, 0)

    def scale(row, carry):
        rows = pl.ds(pl.multiple_of(row * BS, BS), BS)
        delta[rows, :] = (total[row] * slope_ref[rows, :]).astype(BF16)
        return carry

    lax.fori_loop(0, NB, scale, 0, unroll=4)
    out_ref[:, 0:BS] = jnp.dot(summed_ref[...], delta[...], preferred_element_type=F32).astype(BF16)


def last_part(other, back, turned, slope, summed, second):
    return call(
        last_kernel,
        jax.ShapeDtypeStruct((X * BS, (X + 1) * BS), BF16),
        [SMEM] + [VMEM] * 5,
        VMEM,
        [pltpu.VMEM((NB, BS, BS), F32), pltpu.VMEM((ROWS, BS), BF16)],
        (2 * NB * 2 * BS**3 + 2 * ROWS * 512 * BS, 8 * 1024 * 1024, 0),
        "last_part",
    )(other, back, turned, slope, summed, second)


def sum_kernel(got_ref, held_ref, out_ref, passed_ref):
    del held_ref, passed_ref
    rows = got_ref.shape[1]
    second = got_ref[0, :, BS:].astype(F32)
    for k in range(1, X * G):
        second += got_ref[k, :, BS:].astype(F32)
    for x in range(X):
        first = got_ref[x * G, :, :BS].astype(F32)
        for k in range(1, G):
            first += got_ref[x * G + k, :, :BS].astype(F32)
        for z in range(Z):
            out_ref[z, :rows, x * BS : (x + 1) * BS] = first.astype(BF16)
    for z in range(Z):
        out_ref[z, rows:, :] = second.astype(BF16)


def sum_parts(got, held):
    return pl.pallas_call(
        sum_kernel,
        out_shape=(
            jax.ShapeDtypeStruct((Z, 2 * got.shape[1], X * BS), BF16),
            jax.ShapeDtypeStruct(held.shape, held.dtype),
        ),
        in_specs=[VMEM, ANY],
        out_specs=(VMEM, ANY),
        input_output_aliases={1: 1},
        compiler_params=pltpu.CompilerParams(vmem_limit_bytes=LIMIT),
        cost_estimate=pl.CostEstimate(flops=0, bytes_accessed=1024 * 1024, transcendentals=0),
        name="sum_parts",
    )(got, held)


def planes_kernel(parts_ref, after_ref, out_ref):
    del after_ref
    total = parts_ref[0].astype(F32)
    for z in range(1, Z):
        total += parts_ref[z].astype(F32)
    for reader in range(G):
        out_ref[reader] = total.astype(BF16)


def sum_planes(parts, after):
    return call(
        planes_kernel,
        jax.ShapeDtypeStruct((G,) + parts.shape[1:], BF16),
        [VMEM, ANY],
        VMEM,
        [],
        (0, 1024 * 1024, 0),
        "sum_planes",
    )(parts, after)


def assemble_kernel(x_ref, *refs):
    quarters, (out_ref, sem) = refs[:X], refs[X:]
    for k in range(X):
        rows = pl.ds(pl.multiple_of(lax.rem(x_ref[0] + X - k, X) * QUARTER, QUARTER), QUARTER)
        pltpu.make_async_copy(quarters[k], out_ref.at[rows], sem).start()
    pltpu.make_async_copy(out_ref, out_ref, sem).wait()


def assemble(my_x, quarters):
    return call(
        assemble_kernel,
        jax.ShapeDtypeStruct((ROWS, BS), BF16),
        [SMEM] + [VMEM] * X,
        ANY,
        [pltpu.SemaphoreType.DMA],
        (0, 2 * 1024 * 1024, 0),
        "assemble",
    )(my_x, *quarters)


def shift(value, step):
    return lax.ppermute(value, "z", [(i, (i + step) % Z) for i in range(Z)])


def turn(value, step):
    return lax.ppermute(value, "mp", [(i, (i + step) % X) for i in range(X)])


def gather_features(value):
    left, right = turn(value, 1), turn(value, -1)
    half = value.shape[0] // 2
    far = [turn(left[:half], 1), turn(right[half:], -1)]
    return value, left, right, far[0], far[1]


def exchange(value, axes):
    return lax.all_to_all(value, axes, split_axis=0, concat_axis=0, tiled=True)


def plane(staged):
    per = staged.shape[0] // G
    got = exchange(staged.reshape(G, per * BS, BS), ("y", "core"))
    return got.reshape(staged.shape)


def apart(work, my_z, *args):
    def skip(*args):
        return jax.tree.map(lambda leaf: jnp.zeros(leaf.shape, leaf.dtype), shapes)

    shapes = jax.eval_shape(work, *args)
    return lax.cond(my_z < Z, work, skip, *args)


def body(
    input_history,
    hidden_history,
    batch_blocks,
    tile_columns,
    tile_values,
    send_blocks,
    send_counts,
    weight_first,
    weight_second,
    cotangent,
):
    my_z = lax.axis_index("z").astype(jnp.int32)
    my_x = lax.axis_index("mp").astype(jnp.int32)
    blocks = send_blocks[0].T
    other = tile_columns[:, 1]
    table_input = pack(blocks, send_counts, input_history)

    def hop(pair):
        return shift(pair[0], 1), shift(pair[1], -1)

    def far_hop(pair):
        return shift(pair[0][:MIDDLE], 1), shift(pair[1][MIDDLE:], -1)

    def send(*sources, after=()):
        return plane(stage(my_z.reshape(1), [s if isinstance(s, tuple) else (s,) for s in sources], after))

    def beside(*sources, after=()):
        return apart(lambda sources, after: send(*sources, after=after), my_z, sources, after)

    def step_zero(table, blocks, counts, history, first, second):
        weight = jnp.concatenate([first, second])
        return hop((table, table)), beside(table), pack(blocks, counts, history), weight

    def step_one(pair, other):
        return hop(pair), hop((other, other)), beside(*pair, other)

    def step_two(pair, other):
        return hop(pair), hop(other), beside(*pair, *other)

    def step_three(pair, other):
        return far_hop(pair), hop(other), beside(*pair, other[0])

    def step_four(far, other, after):
        return far_hop(other), beside(far, after=after)

    one, piece0, table_hidden, weight = apart(
        step_zero, my_z, table_input, blocks, send_counts, hidden_history, weight_first, weight_second
    )
    weights = lax.all_gather(weight, "mp", axis=0, tiled=False)
    cot = lax.all_gather(cotangent, "mp", axis=0, tiled=False)
    cot_rows = lax.dynamic_slice(cot, (0, my_x * QUARTER, 0), (X, QUARTER, BS))
    order = jnp.stack([my_x, (my_x - 1) % X, (my_x + 1) % X, (my_x + 2) % X])
    columns = lax.dynamic_slice(weights, (0, 0, my_x * BS), (X, BS, BS))[order].reshape(X * BS, BS)
    weight_all = weights[:, BS:].reshape(X * BS, X * BS)

    two, one_hidden, piece1 = apart(step_one, my_z, one, table_hidden)
    three, two_hidden, piece2 = apart(step_two, my_z, two, one_hidden)
    far, three_hidden, piece3 = apart(step_three, my_z, three, two_hidden)
    far_hidden, piece4 = apart(step_four, my_z, far, three_hidden, (weights, cot))

    sides_input = ((0, 0, 1), (1, 1, 3), (2, 1, 4), (3, 1, 3), (4, 0, 1), (3, 0, 3), (2, 0, 4), (1, 0, 3))
    sides_hidden = ((0, 2, 3), (1, 3, 4), (3, 3, 4), (3, 2, 4), (3, 0, 4), (3, 1, 4), (2, 2, 3), (1, 2, 4))
    use = tile_columns[:, 2:] - NB
    owner, slot = use // CAP, use % CAP
    group = (owner // (Z * C)) * C + owner % C
    code = (((owner // C) % Z - my_z) % Z * 256 + group * 8 + slot).reshape(-1)

    batch = batch_blocks.reshape(-1)
    halo_input = (piece0, piece1, piece2, piece3, piece4)
    summed_first = aggregate(sides_input, HEAD, table_input, halo_input, tile_values, code, other, batch)
    piece5 = send(far_hidden, *three_hidden, two_hidden[1], after=(summed_first,))
    halo_hidden = (piece1, piece2, piece3, piece5)
    all_first = gather_features(summed_first)
    hidden_first, slope_first = first_layer(all_first, columns)
    turned_tiles = turn_local(tile_values, summed_first)
    turned_first = prepare(my_x.reshape(1), all_first)
    summed_second = aggregate(sides_hidden, 0, hidden_first, halo_hidden, tile_values, code, other, batch)
    rows_second = exchange(summed_second.reshape(X, QUARTER, BS), "mp")
    out_rows, part_second, back_rows = second_layer(
        my_x.reshape(1), rows_second, weight_all, cot_rows, turned_first
    )
    back_second = exchange(back_rows, "mp").reshape(ROWS, BS)
    got = last_part(other, back_second, turned_tiles, slope_first, turned_first, part_second)

    dealt = X * G
    got = exchange(got.reshape(dealt, -1, (X + 1) * BS), ("mp", "y", "core"))
    parts, out_rows = sum_parts(got, out_rows)
    quarters = [out_rows[0]] + [turn(out_rows[k], k) for k in range(1, X)]
    layer_out = assemble(my_x.reshape(1), quarters)
    both = exchange(sum_planes(exchange(parts, "z"), layer_out), ("y", "core"))
    both = both.reshape(G, 2, -1, X * BS).astype(F32)
    grad_first = both[:, 0].reshape(BS, X * BS)
    grad_second = both[:, 1].reshape(BS, X * BS)
    return (layer_out, grad_first, grad_second)


def solution(mesh):
    inner = Mesh(mesh.devices.reshape(Y, Z, C, X), ("y", "z", "core", "mp"))
    nodes = ("y", "z", "core")
    placed = (
        P(nodes, "mp"),
        P(nodes, "mp"),
        P(nodes, None),
        P(nodes, None),
        P(nodes, None, None, None),
        P(nodes, None, None),
        P(nodes, None),
        P("mp", None),
        P("mp", None),
        P(nodes, "mp"),
    )
    return jax.shard_map(
        body,
        mesh=inner,
        in_specs=placed,
        out_specs=(P(nodes, "mp"), P("mp", None), P("mp", None)),
        check_vma=False,
    )
```
